512 devices in a mesh: dp: 4 (over x), ctx: 8 (over z), expert: 16 (over y, core).
Axes of the slice: x: 4, y: 8, z: 8, core: 2. Of those that a mesh axis runs over, the one named last changes fastest.
Arguments:
- projected: bfloat16 [64, 3, 1024, 1536], P(('dp', 'expert'), None, 'ctx'), may hold values from -6 to 6
- residual_in: bfloat16 [64, 1024, 1536], P(('dp', 'expert'), 'ctx'), may hold values from -6 to 6
- modulation_scale: float32 [64, 1536], P(('dp', 'expert')), may hold values from -3 to 3
- modulation_shift: float32 [64, 1536], P(('dp', 'expert')), may hold values from -3 to 3
- expert_choice: int32 [64, 1024, 2], P(('dp', 'expert'), 'ctx'), may hold values from 0 to 15, all different within a row; in each aligned block of 128 rows (0 to 127, 128 to 255, ..., all dimensions but the last counted through in order) at most 20 rows name the same one
- gate_values: float32 [64, 1024, 2], P(('dp', 'expert'), 'ctx'), may hold values from 0.2 to 1
- expert_in: bfloat16 [16, 3072, 1536], P('expert', ('dp', 'ctx')), may hold values from -0.15625 to 0.15625
- expert_out: bfloat16 [16, 3072, 1536], P('expert', ('dp', 'ctx')), may hold values from -0.109375 to 0.109375
Outputs:
- block_out: bfloat16 [64, 1024, 1536], P(('dp', 'expert'), 'ctx')
The draws below stay inside these ranges and needn't reach their ends.
Inputs may be any that keep to these rules, and one draw needn't show every extreme that they name: `expert_choice`: a token's 2 experts differ; in the rows of one device no expert is named by more than 20 rows, and some device reaches 20.
All inputs are finite; a program needn't handle non-finite values.
Results may differ from the reference program's by a relative error of at most 0.01.
Values may be sent and summed in bfloat16 or wider, within the bound.
No kernel may reach another device: no remote copies, remote signals or barrier semaphores. Data moves between devices by JAX's collectives and lax.ppermute only.
A program may use at most 64 MiB of HBM per device.

```python
import math
import jax
import jax.numpy as jnp
import numpy as np
from jax import lax

D = 1536
HEADS = 24
HD = 64
FFW = 3072
TOP = 2
TOK_DEV = 128
SAMPLES = 64
LEN = 1024
EXPERTS = 16
CAP = 20
N_DP = 4
N_CTX = 8


def draw_projected(key, part):
    base_key = jax.random.fold_in(key, 0)
    shape = (SAMPLES, 3, LEN, D)
    result = jnp.clip(jax.random.normal(base_key, shape, jnp.float32), -6.0, 6.0)
    return result.astype(jnp.bfloat16)


def levels(key, extent, pieces, least, high):
    factor_of, own = 1.0, jax.random.fold_in(key, 6)
    for axis_at, shards_of in pieces:
        draws = jnp.exp(jax.random.uniform(jax.random.fold_in(own, axis_at), (shards_of,), jnp.float32, least / len(pieces), high / len(pieces)))
        factor_of = factor_of * jnp.repeat(draws, extent[axis_at] // shards_of).reshape([-1 if axis == axis_at else 1 for axis in range(len(extent))])
    return factor_of


def assign_block(stream_key, own, number, rows, count, top, limit, skew):
    order = jax.random.permutation(stream_key, count)
    packed, common = portions_of(count, rows * top, limit, skew, True), portions_of(count, rows * top, limit, skew, False)
    places = jnp.arange(count)

    def named(lengths, turn):
        used = int((lengths > 0).sum())
        fixed = max(1, used // 4)
        moved = fixed + (places - fixed + turn * (used - fixed)) % max(1, count - fixed)
        return jnp.zeros((count,), jnp.int32).at[order[jnp.where(places < fixed, places, moved)]].set(jnp.asarray(lengths, jnp.int32))

    lengths = jnp.where(number % 4 == 0, named(packed, number // 4), named(common, number - number // 4 - 1))
    mixed = jax.random.permutation(jax.random.fold_in(own, 3), count)
    giver, sink = mixed[0:count // 2 * 2:2], mixed[1:count // 2 * 2:2]
    slack = jnp.minimum(lengths[giver] - 1, limit - lengths[sink]) // 2
    slack = jnp.where((giver == order[0]) | (sink == order[0]) | (lengths[sink] == 0), 0, jnp.maximum(slack, 0))
    moved = jax.random.randint(jax.random.fold_in(own, 4), (count // 2,), 0, 1 << 20) % (slack + 1)
    lengths = lengths.at[giver].add(-moved).at[sink].add(moved)
    members = jnp.searchsorted(jnp.cumsum(lengths), jnp.arange(rows * top), side="right").astype(jnp.int32)
    grid = members.reshape(top, rows).T
    grid = grid[jax.random.permutation(jax.random.fold_in(own, 1), rows)]
    turn = jax.random.randint(jax.random.fold_in(own, 2), (rows, 1), 0, top)
    return jnp.take_along_axis(grid, (jnp.arange(top)[None, :] + turn) % top, axis=1)


def portions_of(count, total, most, skew, full):
    loads = [(1 << 20) // math.isqrt(grade ** skew) + 1 for grade in range(1, count + 1)]
    largest = most if full else min(most, max(-(-total // count), total * loads[0] // sum(loads)))
    least = 1 if total - largest >= count - 1 else 0
    counts, spare = [largest] + [least] * (count - 1), total - largest - least * (count - 1)
    while spare > 0:
        candidates = [i for i in range(1, count) if counts[i] < largest] or [i for i in range(1, count) if counts[i] < most]
        pool, budget = sum([loads[i] for i in candidates]), spare
        for i in candidates:
            more = min(most - counts[i], max(1, budget * loads[i] // pool), spare)
            counts[i] = counts[i] + more
            spare = spare - more
    return np.array(counts)


def bell_draw(rng, dims, width, reach, shards=(), kind=jnp.bfloat16):
    drawn = width * jax.random.normal(rng, dims, jnp.float32)
    if shards:
        drawn = drawn * levels(rng, dims, shards, -0.22, 0.18)
    return jnp.clip(drawn, -reach, reach).astype(kind)


def setup_inputs(seed: int = 0) -> dict:
    key_of = jax.random.split(jax.random.key(seed), 9)
    projected = draw_projected(jax.random.fold_in(key_of[8], 71), 0)
    residual_in = bell_draw(key_of[1], (SAMPLES, LEN, D), 1.0, 6.0, ((0, 64), (1, 8)))
    modulation_scale = bell_draw(key_of[2], (SAMPLES, D), 0.5, 3.0, ((0, 64),), jnp.float32)
    modulation_shift = bell_draw(key_of[3], (SAMPLES, D), 0.5, 3.0, ((0, 64),), jnp.float32)
    expert_choice_keys = jax.random.split(jax.random.fold_in(key_of[4], 1), SAMPLES * LEN // TOK_DEV)
    expert_choice_turns = jax.random.permutation(jax.random.fold_in(key_of[4], 3), SAMPLES * LEN // TOK_DEV)
    expert_choice = jax.vmap(lambda own, number: assign_block(jax.random.fold_in(key_of[4], 2), own, number, TOK_DEV, EXPERTS, TOP, CAP, 1))(expert_choice_keys, expert_choice_turns).reshape((SAMPLES, LEN, TOP))
    gate_values = jnp.clip(0.2 + 0.8 * jax.random.uniform(key_of[5], (SAMPLES, LEN, TOP), jnp.float32) ** levels(key_of[5], (SAMPLES, LEN, TOP), ((0, 64), (1, 8)), -0.2, 0.2), 0.2, 1.0)
    expert_in = bell_draw(key_of[6], (EXPERTS, FFW, D), D ** -0.5, 0.15625, ((0, 16), (1, 32)))
    expert_out = bell_draw(key_of[7], (EXPERTS, FFW, D), FFW ** -0.5, 0.109375, ((0, 16), (1, 32)))
    return {"projected": projected, "residual_in": residual_in, "modulation_scale": modulation_scale, "modulation_shift": modulation_shift, "expert_choice": expert_choice, "gate_values": gate_values, "expert_in": expert_in, "expert_out": expert_out}


def attend_sample(sample):
    queries = sample[0].reshape(LEN, HEADS, HD).astype(jnp.float32)
    keys_all = sample[1].reshape(LEN, HEADS, HD).astype(jnp.float32)
    values_all = sample[2].reshape(LEN, HEADS, HD).astype(jnp.float32)
    scores = jnp.einsum('qhd,khd->hqk', queries, keys_all) * HD ** (-0.5)
    top_score = lax.optimization_barrier(jnp.max(scores, axis=-1, keepdims=True))
    probs = jnp.exp(scores - top_score)
    totals = lax.optimization_barrier(jnp.sum(probs, axis=-1))
    rounded = probs.astype(jnp.bfloat16).astype(jnp.float32)
    mixed = jnp.einsum('hqk,khd->qhd', rounded, values_all) / jnp.transpose(totals)[:, :, None]
    return mixed.reshape(LEN, D).astype(jnp.bfloat16)

def slot_numbers(choice_row):
    onehot = (choice_row[:, None] == jnp.arange(EXPERTS, dtype=jnp.int32)[None, :]).astype(jnp.int32)
    before = jnp.cumsum(onehot, axis=0) - onehot
    position = lax.optimization_barrier(jnp.sum(before * onehot, axis=1))
    return (choice_row * CAP + position).astype(jnp.int32)

def run_expert(operands):
    routed, weight_in, weight_out = operands
    slice_size = FFW // N_DP
    total = jnp.zeros((routed.shape[0], D), jnp.float32)
    for slice_index in range(N_DP):
        rows_in = weight_in[slice_index * slice_size:(slice_index + 1) * slice_size]
        rows_out = weight_out[slice_index * slice_size:(slice_index + 1) * slice_size]
        pre_act = jnp.dot(routed, jnp.transpose(rows_in), preferred_element_type=jnp.float32)
        hidden = jax.nn.gelu(pre_act, approximate=True).astype(jnp.bfloat16)
        partial_sum = jnp.dot(hidden, rows_out, preferred_element_type=jnp.float32).astype(jnp.bfloat16)
        partial_sum = lax.optimization_barrier(partial_sum)
        total = total + partial_sum.astype(jnp.float32)
    return total.astype(jnp.bfloat16)

def reference(projected, residual_in, modulation_scale, modulation_shift, expert_choice, gate_values, expert_in, expert_out):
    attended = lax.map(attend_sample, projected)
    stream = residual_in.astype(jnp.float32) + attended.astype(jnp.float32)
    mean_square = lax.optimization_barrier(jnp.mean(stream * stream, axis=-1, keepdims=True))
    normed = stream / jnp.sqrt(mean_square + 1e-06) * (1.0 + modulation_scale[:, None, :]) + modulation_shift[:, None, :]
    normed = normed.astype(jnp.bfloat16)
    blocks = SAMPLES * N_CTX
    normed_blocks = normed.reshape(blocks, TOK_DEV, D)
    choices_flat = expert_choice.reshape(blocks, TOK_DEV * TOP).astype(jnp.int32)
    targets = jax.vmap(slot_numbers)(choices_flat)
    pair_rows = jnp.repeat(normed_blocks, TOP, axis=1)

    def fill_buffer(target_row, values_row):
        return jnp.zeros((EXPERTS * CAP, D), jnp.bfloat16).at[target_row].set(values_row)
    buffers = jax.vmap(fill_buffer)(targets, pair_rows)
    per_expert = jnp.transpose(buffers.reshape(blocks, EXPERTS, CAP, D), (1, 0, 2, 3)).reshape(EXPERTS, blocks * CAP, D)
    results = lax.map(run_expert, (per_expert, expert_in, expert_out))
    returned = jnp.transpose(results.reshape(EXPERTS, blocks, CAP, D), (1, 0, 2, 3)).reshape(blocks, EXPERTS * CAP, D)
    picked = jax.vmap(lambda table, target_row: table[target_row])(returned, targets)
    picked = picked.reshape(blocks, TOK_DEV, TOP, D).astype(jnp.float32)
    gates = gate_values.reshape(blocks, TOK_DEV, TOP)
    mixture = lax.optimization_barrier(jnp.sum(gates[..., None] * picked, axis=2))
    result = stream.reshape(blocks, TOK_DEV, D) + mixture
    return result.astype(jnp.bfloat16).reshape(SAMPLES, LEN, D)
```

```python
import functools

import jax
import jax.numpy as jnp
from jax import lax
from jax.experimental import pallas as pl
from jax.experimental.pallas import tpu as pltpu
from jax.sharding import PartitionSpec as P

HD = 64
CHUNKS = 1
BF = jnp.bfloat16
F32 = jnp.float32
LIMIT = 48 * 1024 * 1024


def swap(x):
    return jnp.concatenate([x[:, HD:], x[:, :HD]], axis=1)


def low_lanes(rows):
    return lax.broadcasted_iota(jnp.int32, (rows, 2 * HD), 1) < HD


def pack_kernel(x_ref, o_ref):
    n = o_ref.shape[0]
    t = x_ref.shape[2]
    half = t // 2
    low, low_half = low_lanes(t), low_lanes(half)
    for j in range(n):
        for part in range(3):
            o_ref[j, part * t : (part + 1) * t, :] = x_ref[0, part, :, 128 * j : 128 * (j + 1)]
        at = 128 * (n + j // 2)
        q, k, v = (x_ref[0, part, :, at : at + 128] for part in range(3))
        if j % 2 == 0:
            o_ref[j, 3 * t : 4 * t, :] = jnp.where(low, q, swap(k))
            o_ref[j, 4 * t :, :] = jnp.where(low_half, v[:half], swap(v[half:]))
        else:
            o_ref[j, 3 * t : 4 * t, :] = jnp.where(low, swap(q), k)
            o_ref[j, 4 * t :, :] = jnp.where(low_half, swap(v[:half]), v[half:])


def attend_kernel(m_ref, o_ref, v2_ref):
    n, _, _ = m_ref.shape
    t = m_ref.shape[1] * 2 // 9
    half = t // 2
    group = o_ref.shape[0]
    step = pl.program_id(0)

    @pl.when(step == 0)
    def _():
        for z in range(n):
            block = m_ref[z, 4 * t :, :]
            v2_ref[z * t : z * t + half, :] = block
            v2_ref[z * t + half : (z + 1) * t, :] = swap(block)

    rows = group * t
    low = low_lanes(rows)
    mine = pl.ds(step * group, group)
    q01 = m_ref[mine, 0:t, :].reshape(rows, 128)
    q2 = swap(m_ref[mine, 3 * t : 4 * t, :].reshape(rows, 128))
    k01 = m_ref[:, t : 2 * t, :].reshape(n * t, 128)
    k2 = m_ref[:, 3 * t : 4 * t, :].reshape(n * t, 128)
    v01 = m_ref[:, 2 * t : 3 * t, :].reshape(n * t, 128)
    v2 = v2_ref[...]
    zero = jnp.zeros_like(q01)

    def head(q, k, v):
        scores = lax.dot_general(q, k, (((1,), (1,)), ((), ())), preferred_element_type=F32)
        scores = scores * HD ** (-0.5)
        probs = jnp.exp(scores - jnp.max(scores, axis=-1, keepdims=True))
        totals = jnp.sum(probs, axis=-1, keepdims=True)
        return jnp.dot(probs.astype(BF), v, preferred_element_type=F32) / totals

    a = head(jnp.where(low, q01, zero), k01, v01)
    b = head(jnp.where(low, zero, q01), k01, v01)
    c = head(jnp.where(low, zero, q2), k2, v2).astype(BF)
    pair = jnp.where(low, a, b).astype(BF)
    low_half = low_lanes(half)
    for g in range(group):
        o_ref[g, 0:t, :] = pair[g * t : (g + 1) * t]
        o_ref[g, t:, :] = jnp.where(
            low_half, c[g * t : g * t + half], swap(c[g * t + half : (g + 1) * t])
        )


def dispatch_kernel(experts, cap, b_ref, r_ref, scale_ref, shift_ref, choice_ref, s_ref, *sends):
    n = b_ref.shape[0]
    t, width = r_ref.shape
    half = t // 2
    low_half = low_lanes(half)
    tiles = [b_ref[j, 0:t, :] for j in range(n)]
    for m in range(n // 2):
        even, odd = b_ref[2 * m, t:, :], b_ref[2 * m + 1, t:, :]
        top = jnp.where(low_half, even, swap(odd))
        bottom = jnp.where(low_half, swap(even), odd)
        tiles.append(jnp.concatenate([top, bottom], axis=0))
    attended = jnp.concatenate(tiles, axis=1)
    stream = r_ref[...].astype(F32) + attended.astype(F32)
    s_ref[...] = stream
    mean_square = jnp.mean(stream * stream, axis=-1, keepdims=True)
    normed = (
        stream / jnp.sqrt(mean_square + 1e-06) * (1.0 + scale_ref[...]) + shift_ref[...]
    ).astype(BF)
    choices = choice_ref[...]
    expert_at = lax.broadcasted_iota(jnp.int32, (experts, t), 0)
    first, second = expert_at == choices[0:1], expert_at == choices[1:2]
    earlier = lax.broadcasted_iota(jnp.int32, (t, t), 0) < lax.broadcasted_iota(
        jnp.int32, (t, t), 1
    )
    before = jnp.dot(
        (first | second).astype(F32).astype(BF),
        earlier.astype(F32).astype(BF),
        preferred_element_type=F32,
    ).astype(jnp.int32)
    keys = [
        choices[k : k + 1] * 32 + jnp.sum(jnp.where(named, before, 0), axis=0, keepdims=True)
        for k, named in enumerate((first, second))
    ]
    part = cap // len(sends)
    main, extra = part * 4 // 5, part // 5
    rows = experts * main
    at = lax.broadcasted_iota(jnp.int32, (rows, 1), 0)
    quarter = width // 4
    for c, send in enumerate(sends):
        main_key = at // main * 32 + c * part + at % main
        pick = ((main_key == keys[0]) | (main_key == keys[1])).astype(F32).astype(BF)
        send[:, :width] = jnp.dot(pick, normed, preferred_element_type=F32).astype(BF)
        extra_key = at // main * 32 + c * part + main + at % main // 4
        matches = (extra_key == keys[0]) | (extra_key == keys[1])
        total = jnp.zeros((rows, quarter), F32)
        for q in range(4):
            pick = (matches & (at % 4 == q)).astype(F32).astype(BF)
            total += jnp.dot(
                pick, normed[:, q * quarter : (q + 1) * quarter], preferred_element_type=F32
            )
        send[:, width:] = total.astype(BF)


def expert_kernel(x_ref, in_ref, out_ref, y_ref, rows_ref):
    rows = x_ref.shape[0]
    width = in_ref.shape[1]
    quarter = width // 4
    extras = rows // 4
    rows_ref[:rows, :] = x_ref[:, :width]
    packed = x_ref[:, width:]
    row_at = lax.broadcasted_iota(jnp.int32, (extras, rows), 0)
    source = lax.broadcasted_iota(jnp.int32, (extras, rows), 1)
    for q in range(4):
        pick = (source == 4 * row_at + q).astype(F32).astype(BF)
        rows_ref[rows:, q * quarter : (q + 1) * quarter] = jnp.dot(
            pick, packed, preferred_element_type=F32
        ).astype(BF)
    pre_act = lax.dot_general(
        rows_ref[...], in_ref[...], (((1,), (1,)), ((), ())), preferred_element_type=F32
    )
    hidden = jax.nn.gelu(pre_act, approximate=True).astype(BF)
    partial = jnp.dot(hidden, out_ref[...], preferred_element_type=F32).astype(BF)
    y_ref[:, :width] = partial[:rows]
    to = lax.broadcasted_iota(jnp.int32, (rows, extras), 0)
    origin = lax.broadcasted_iota(jnp.int32, (rows, extras), 1)
    total = jnp.zeros((rows, quarter), F32)
    for q in range(4):
        pick = (to == 4 * origin + q).astype(F32).astype(BF)
        total += jnp.dot(
            pick, partial[rows:, q * quarter : (q + 1) * quarter], preferred_element_type=F32
        )
    y_ref[:, width:] = total.astype(BF)


def combine_kernel(experts, cap, s_ref, choice_ref, gate_ref, *refs):
    returned, o_ref = refs[:-1], refs[-1]
    t, width = s_ref.shape
    choices = choice_ref[...]
    expert_at = lax.broadcasted_iota(jnp.int32, (t, 128), 1)
    first, second = expert_at == choices[:, 0:1], expert_at == choices[:, 1:2]
    earlier = lax.broadcasted_iota(jnp.int32, (t, t), 1) < lax.broadcasted_iota(
        jnp.int32, (t, t), 0
    )
    before = jnp.dot(
        earlier.astype(F32).astype(BF),
        (first | second).astype(F32).astype(BF),
        preferred_element_type=F32,
    ).astype(jnp.int32)
    keys = jnp.concatenate(
        [
            choices[:, k : k + 1] * 32
            + jnp.sum(jnp.where(named, before, 0), axis=1, keepdims=True)
            for k, named in enumerate((first, second))
        ],
        axis=0,
    )
    part = cap // len(returned)
    main, extra = part * 4 // 5, part // 5
    rows = experts * main
    at = lax.broadcasted_iota(jnp.int32, (1, rows), 1)
    quarter = width // 4
    picked = jnp.zeros((2 * t, width), F32)
    for c, back in enumerate(returned):
        main_key = at // main * 32 + c * part + at % main
        pick = (main_key == keys).astype(F32).astype(BF)
        picked += jnp.dot(pick, back[:, :width], preferred_element_type=F32)
        extra_key = at // main * 32 + c * part + main + at % main // 4
        parts = []
        for q in range(4):
            pick = ((extra_key == keys) & (at % 4 == q)).astype(F32).astype(BF)
            parts.append(jnp.dot(pick, back[:, width:], preferred_element_type=F32))
        picked += jnp.concatenate(parts, axis=1)
    gates = gate_ref[...]
    mixture = gates[:, 0:1] * picked[:t] + gates[:, 1:2] * picked[t:]
    o_ref[0] = (s_ref[...] + mixture).astype(BF)


def local(kernel, out_shape, scratch=(), **more):
    return pl.pallas_call(
        kernel,
        out_shape=out_shape,
        scratch_shapes=scratch,
        compiler_params=pltpu.CompilerParams(vmem_limit_bytes=LIMIT),
        **more,
    )


def run_experts(x, weight_in, weight_out):
    rows, wide = x.shape
    hidden, width = weight_in.shape
    work = rows * 5 // 4
    return local(
        expert_kernel,
        jax.ShapeDtypeStruct((rows, wide), BF),
        [pltpu.VMEM((work, width), BF)],
        cost_estimate=pl.CostEstimate(
            flops=4 * work * hidden * width,
            bytes_accessed=4 * hidden * width + 4 * rows * wide,
            transcendentals=work * hidden,
        ),
    )(x, weight_in, weight_out)


def add(a, b):
    return (a.astype(F32) + b.astype(F32)).astype(BF)


def expert_layer(x, weights):
    right = [(i, (i + 1) % 4) for i in range(4)]
    left = [(i, (i + 3) % 4) for i in range(4)]
    half = x.shape[0] // 2
    from_left = lax.ppermute(x, "dp", right)
    from_right = lax.ppermute(x, "dp", left)
    across = jnp.concatenate(
        [
            lax.ppermute(from_left[:half], "dp", right),
            lax.ppermute(from_right[half:], "dp", left),
        ]
    )
    own = run_experts(x, *weights)
    for_left = run_experts(from_left, *weights)
    for_right = run_experts(from_right, *weights)
    for_across = run_experts(across, *weights)
    via_left = lax.ppermute(for_across[:half], "dp", right)
    via_right = lax.ppermute(for_across[half:], "dp", left)
    to_right = jnp.concatenate([add(for_right[:half], via_left), for_right[half:]])
    to_left = jnp.concatenate([for_left[:half], add(for_left[half:], via_right)])
    one = lax.ppermute(to_right, "dp", right)
    two = lax.ppermute(to_left, "dp", left)
    return (own.astype(F32) + one.astype(F32) + two.astype(F32)).astype(BF)


def per_device(
    projected,
    residual_in,
    modulation_scale,
    modulation_shift,
    expert_choice,
    gate_values,
    expert_in,
    expert_out,
):
    _, _, t, width = projected.shape
    n = lax.axis_size("ctx")
    experts = lax.axis_size("expert")
    cap = 5 * t * 2 // (4 * experts)
    packed = local(pack_kernel, jax.ShapeDtypeStruct((n, t * 9 // 2, 128), BF))(projected)
    mixed = lax.all_to_all(packed, "ctx", 0, 0, tiled=True)
    mixed, expert_in, expert_out = lax.optimization_barrier((mixed, expert_in, expert_out))
    weights = (
        lax.all_gather(expert_in[0], "ctx", axis=0, tiled=True),
        lax.all_gather(expert_out[0], "ctx", axis=0, tiled=True),
    )
    group = 2
    head_output = local(
        attend_kernel,
        jax.ShapeDtypeStruct((n, t * 3 // 2, 128), BF),
        [pltpu.VMEM((n * t, 128), BF)],
        grid=(n // group,),
        in_specs=[pl.BlockSpec((n, t * 9 // 2, 128), lambda i: (0, 0, 0))],
        out_specs=pl.BlockSpec((group, t * 3 // 2, 128), lambda i: (i, 0, 0)),
    )(mixed)
    back = lax.all_to_all(head_output, "ctx", 0, 0, tiled=True)
    part = cap // CHUNKS
    wide = (experts * part * 4 // 5, width * 5 // 4)
    stream, *sends = local(
        functools.partial(dispatch_kernel, experts, cap),
        [jax.ShapeDtypeStruct((t, width), F32)] + [jax.ShapeDtypeStruct(wide, BF)] * CHUNKS,
    )(back, residual_in[0], modulation_scale, modulation_shift, expert_choice[0].T)
    arrived = [lax.all_to_all(x, "expert", 0, 0, tiled=True) for x in sends]
    sums = [expert_layer(x, weights) for x in arrived]
    returned = [lax.all_to_all(x, "expert", 0, 0, tiled=True) for x in sums]
    return local(
        functools.partial(combine_kernel, experts, cap),
        jax.ShapeDtypeStruct((1, t, width), BF),
    )(stream, expert_choice[0], gate_values[0], *returned)


def solution(mesh):
    return jax.shard_map(
        per_device,
        mesh=mesh,
        in_specs=(
            P(("dp", "expert"), None, "ctx", None),
            P(("dp", "expert"), "ctx", None),
            P(("dp", "expert"), None),
            P(("dp", "expert"), None),
            P(("dp", "expert"), "ctx", None),
            P(("dp", "expert"), "ctx", None),
            P("expert", ("dp", "ctx"), None),
            P("expert", ("dp", "ctx"), None),
        ),
        out_specs=P(("dp", "expert"), "ctx", None),
        check_vma=False,
    )
```

```python
import functools

import jax
import jax.numpy as jnp
from jax import lax
from jax.experimental import pallas as pl
from jax.experimental.pallas import tpu as pltpu
from jax.sharding import PartitionSpec as P

HD = 64
CHUNKS = 1
BF = jnp.bfloat16
F32 = jnp.float32
LIMIT = 48 * 1024 * 1024


def swap(x):
    return jnp.concatenate([x[:, HD:], x[:, :HD]], axis=1)


def low_lanes(rows):
    return lax.broadcasted_iota(jnp.int32, (rows, 2 * HD), 1) < HD


def pack_kernel(x_ref, in_ref, out_ref, o_ref, w_ref):
    w_ref[: in_ref.shape[1], :] = in_ref[0]
    w_ref[in_ref.shape[1] :, :] = out_ref[0]
    n = o_ref.shape[0]
    t = x_ref.shape[2]
    half = t // 2
    low, low_half = low_lanes(t), low_lanes(half)
    for j in range(n):
        for part in range(3):
            o_ref[j, part * t : (part + 1) * t, :] = x_ref[0, part, :, 128 * j : 128 * (j + 1)]
        at = 128 * (n + j // 2)
        q, k, v = (x_ref[0, part, :, at : at + 128] for part in range(3))
        if j % 2 == 0:
            o_ref[j, 3 * t : 4 * t, :] = jnp.where(low, q, swap(k))
            o_ref[j, 4 * t :, :] = jnp.where(low_half, v[:half], swap(v[half:]))
        else:
            o_ref[j, 3 * t : 4 * t, :] = jnp.where(low, swap(q), k)
            o_ref[j, 4 * t :, :] = jnp.where(low_half, swap(v[:half]), v[half:])


def attend_kernel(m_ref, o_ref, v2_ref):
    n, _, _ = m_ref.shape
    t = m_ref.shape[1] * 2 // 9
    half = t // 2
    group = o_ref.shape[0]
    step = pl.program_id(0)

    @pl.when(step == 0)
    def _():
        for z in range(n):
            block = m_ref[z, 4 * t :, :]
            v2_ref[z * t : z * t + half, :] = block
            v2_ref[z * t + half : (z + 1) * t, :] = swap(block)

    rows = group * t
    low = low_lanes(rows)
    mine = pl.ds(step * group, group)
    q01 = m_ref[mine, 0:t, :].reshape(rows, 128)
    q2 = swap(m_ref[mine, 3 * t : 4 * t, :].reshape(rows, 128))
    k01 = m_ref[:, t : 2 * t, :].reshape(n * t, 128)
    k2 = m_ref[:, 3 * t : 4 * t, :].reshape(n * t, 128)
    v01 = m_ref[:, 2 * t : 3 * t, :].reshape(n * t, 128)
    v2 = v2_ref[...]
    zero = jnp.zeros_like(q01)

    def head(q, k, v):
        scores = lax.dot_general(q, k, (((1,), (1,)), ((), ())), preferred_element_type=F32)
        scores = scores * HD ** (-0.5)
        probs = jnp.exp(scores - jnp.max(scores, axis=-1, keepdims=True))
        totals = jnp.sum(probs, axis=-1, keepdims=True)
        return jnp.dot(probs.astype(BF), v, preferred_element_type=F32) / totals

    a = head(jnp.where(low, q01, zero), k01, v01)
    b = head(jnp.where(low, zero, q01), k01, v01)
    c = head(jnp.where(low, zero, q2), k2, v2).astype(BF)
    pair = jnp.where(low, a, b).astype(BF)
    low_half = low_lanes(half)
    for g in range(group):
        o_ref[g, 0:t, :] = pair[g * t : (g + 1) * t]
        o_ref[g, t:, :] = jnp.where(
            low_half, c[g * t : g * t + half], swap(c[g * t + half : (g + 1) * t])
        )


def dispatch_kernel(experts, cap, b_ref, r_ref, scale_ref, shift_ref, choice_ref, s_ref, *sends):
    n = b_ref.shape[0]
    t, width = r_ref.shape
    half = t // 2
    low_half = low_lanes(half)
    tiles = [b_ref[j, 0:t, :] for j in range(n)]
    for m in range(n // 2):
        even, odd = b_ref[2 * m, t:, :], b_ref[2 * m + 1, t:, :]
        top = jnp.where(low_half, even, swap(odd))
        bottom = jnp.where(low_half, swap(even), odd)
        tiles.append(jnp.concatenate([top, bottom], axis=0))
    attended = jnp.concatenate(tiles, axis=1)
    stream = r_ref[...].astype(F32) + attended.astype(F32)
    s_ref[...] = stream
    mean_square = jnp.mean(stream * stream, axis=-1, keepdims=True)
    normed = (
        stream / jnp.sqrt(mean_square + 1e-06) * (1.0 + scale_ref[...]) + shift_ref[...]
    ).astype(BF)
    choices = choice_ref[...]
    expert_at = lax.broadcasted_iota(jnp.int32, (experts, t), 0)
    first, second = expert_at == choices[0:1], expert_at == choices[1:2]
    earlier = lax.broadcasted_iota(jnp.int32, (t, t), 0) < lax.broadcasted_iota(
        jnp.int32, (t, t), 1
    )
    before = jnp.dot(
        (first | second).astype(F32).astype(BF),
        earlier.astype(F32).astype(BF),
        preferred_element_type=F32,
    ).astype(jnp.int32)
    keys = [
        choices[k : k + 1] * 32 + jnp.sum(jnp.where(named, before, 0), axis=0, keepdims=True)
        for k, named in enumerate((first, second))
    ]
    part = cap // len(sends)
    main, extra = part * 4 // 5, part // 5
    rows = experts * main
    at = lax.broadcasted_iota(jnp.int32, (rows, 1), 0)
    quarter = width // 4
    for c, send in enumerate(sends):
        main_key = at // main * 32 + c * part + at % main
        pick = ((main_key == keys[0]) | (main_key == keys[1])).astype(F32).astype(BF)
        send[:, :width] = jnp.dot(pick, normed, preferred_element_type=F32).astype(BF)
        extra_key = at // main * 32 + c * part + main + at % main // 4
        matches = (extra_key == keys[0]) | (extra_key == keys[1])
        total = jnp.zeros((rows, quarter), F32)
        for q in range(4):
            pick = (matches & (at % 4 == q)).astype(F32).astype(BF)
            total += jnp.dot(
                pick, normed[:, q * quarter : (q + 1) * quarter], preferred_element_type=F32
            )
        send[:, width:] = total.astype(BF)


def assemble_kernel(*refs):
    blocks, (in_ref, out_ref) = refs[:-2], refs[-2:]
    rows = in_ref.shape[0] // len(blocks)
    for i, block in enumerate(blocks):
        in_ref[i * rows : (i + 1) * rows, :] = block[:rows, :]
        out_ref[i * rows : (i + 1) * rows, :] = block[rows:, :]


def expert_kernel(pieces, in_ref, out_ref, *refs):
    x_refs, y_refs, rows_ref = refs[:pieces], refs[pieces:-1], refs[-1]
    rows = x_refs[0].shape[0]
    width = in_ref.shape[1]
    quarter = width // 4
    extras = rows // 4
    every = rows + extras
    row_at = lax.broadcasted_iota(jnp.int32, (extras, rows), 0)
    source = lax.broadcasted_iota(jnp.int32, (extras, rows), 1)
    picks = [(source == 4 * row_at + q).astype(F32).astype(BF) for q in range(4)]
    for p, x_ref in enumerate(x_refs):
        base = p * every
        rows_ref[base : base + rows, :] = x_ref[:, :width]
        packed = x_ref[:, width:]
        for q in range(4):
            rows_ref[base + rows : base + every, q * quarter : (q + 1) * quarter] = jnp.dot(
                picks[q], packed, preferred_element_type=F32
            ).astype(BF)
    pre_act = lax.dot_general(
        rows_ref[...], in_ref[...], (((1,), (1,)), ((), ())), preferred_element_type=F32
    )
    hidden = jax.nn.gelu(pre_act, approximate=True).astype(BF)
    partial = jnp.dot(hidden, out_ref[...], preferred_element_type=F32).astype(BF)
    to = lax.broadcasted_iota(jnp.int32, (rows, extras), 0)
    origin = lax.broadcasted_iota(jnp.int32, (rows, extras), 1)
    picks = [(to == 4 * origin + q).astype(F32).astype(BF) for q in range(4)]
    for p, y_ref in enumerate(y_refs):
        base = p * every
        y_ref[:, :width] = partial[base : base + rows]
        total = jnp.zeros((rows, quarter), F32)
        for q in range(4):
            total += jnp.dot(
                picks[q],
                partial[base + rows : base + every, q * quarter : (q + 1) * quarter],
                preferred_element_type=F32,
            )
        y_ref[:, width:] = total.astype(BF)


def combine_kernel(experts, cap, s_ref, choice_ref, gate_ref, *refs):
    returned, o_ref = refs[:-1], refs[-1]
    t, width = s_ref.shape
    choices = choice_ref[...]
    expert_at = lax.broadcasted_iota(jnp.int32, (t, 128), 1)
    first, second = expert_at == choices[:, 0:1], expert_at == choices[:, 1:2]
    earlier = lax.broadcasted_iota(jnp.int32, (t, t), 1) < lax.broadcasted_iota(
        jnp.int32, (t, t), 0
    )
    before = jnp.dot(
        earlier.astype(F32).astype(BF),
        (first | second).astype(F32).astype(BF),
        preferred_element_type=F32,
    ).astype(jnp.int32)
    keys = jnp.concatenate(
        [
            choices[:, k : k + 1] * 32
            + jnp.sum(jnp.where(named, before, 0), axis=1, keepdims=True)
            for k, named in enumerate((first, second))
        ],
        axis=0,
    )
    part = cap // len(returned)
    main, extra = part * 4 // 5, part // 5
    rows = experts * main
    at = lax.broadcasted_iota(jnp.int32, (1, rows), 1)
    quarter = width // 4
    picked = jnp.zeros((2 * t, width), F32)
    for c, back in enumerate(returned):
        main_key = at // main * 32 + c * part + at % main
        pick = (main_key == keys).astype(F32).astype(BF)
        picked += jnp.dot(pick, back[:, :width], preferred_element_type=F32)
        extra_key = at // main * 32 + c * part + main + at % main // 4
        parts = []
        for q in range(4):
            pick = ((extra_key == keys) & (at % 4 == q)).astype(F32).astype(BF)
            parts.append(jnp.dot(pick, back[:, width:], preferred_element_type=F32))
        picked += jnp.concatenate(parts, axis=1)
    gates = gate_ref[...]
    mixture = gates[:, 0:1] * picked[:t] + gates[:, 1:2] * picked[t:]
    o_ref[0] = (s_ref[...] + mixture).astype(BF)


def local(kernel, out_shape, scratch=(), **more):
    return pl.pallas_call(
        kernel,
        out_shape=out_shape,
        scratch_shapes=scratch,
        compiler_params=pltpu.CompilerParams(vmem_limit_bytes=LIMIT),
        **more,
    )


def run_experts(pieces, weight_in, weight_out):
    rows, wide = pieces[0].shape
    hidden, width = weight_in.shape
    work = len(pieces) * rows * 5 // 4
    return local(
        functools.partial(expert_kernel, len(pieces)),
        [jax.ShapeDtypeStruct((rows, wide), BF)] * len(pieces),
        [pltpu.VMEM((work, width), BF)],
        cost_estimate=pl.CostEstimate(
            flops=4 * work * hidden * width,
            bytes_accessed=4 * hidden * width + 4 * len(pieces) * rows * wide,
            transcendentals=work * hidden,
        ),
    )(weight_in, weight_out, *pieces)


def add(*parts):
    return sum(p.astype(F32) for p in parts).astype(BF)


def shift(x, axis, by):
    n = lax.axis_size(axis)
    return lax.ppermute(x, axis, [(i, (i + by) % n) for i in range(n)])


def after(x, *others):
    return lax.optimization_barrier((x, *others))[0]


def expert_layer(x, weights):
    half = x.shape[0] // 2
    a, b = x[:half], x[half:]
    left_a, right_b = shift(a, "dp", 1), shift(b, "dp", -1)
    left_b, right_a = shift(b, "dp", 1), shift(a, "dp", -1)
    across_a, across_b = shift(left_a, "dp", 1), shift(right_b, "dp", -1)
    to_left_a, to_left_b, to_right_a, to_right_b = run_experts(
        [left_a, left_b, right_a, right_b], *weights
    )
    got_a, got_b = shift(to_left_a, "dp", -1), shift(to_right_b, "dp", 1)
    to_across_a, to_across_b = run_experts([across_a, across_b], *weights)
    via_a, via_b = shift(to_across_a, "dp", 1), shift(to_across_b, "dp", -1)
    own_a, own_b = run_experts([a, b], *weights)
    sum_a = shift(add(to_right_a, via_a), "dp", 1)
    sum_b = shift(add(to_left_b, via_b), "dp", -1)
    return jnp.concatenate([add(own_a, got_a, sum_a), add(own_b, got_b, sum_b)])


def per_device(
    projected,
    residual_in,
    modulation_scale,
    modulation_shift,
    expert_choice,
    gate_values,
    expert_in,
    expert_out,
):
    _, _, t, width = projected.shape
    n = lax.axis_size("ctx")
    experts = lax.axis_size("expert")
    cap = 5 * t * 2 // (4 * experts)
    slice_rows = expert_in.shape[1]
    packed, block = local(
        pack_kernel,
        [
            jax.ShapeDtypeStruct((n, t * 9 // 2, 128), BF),
            jax.ShapeDtypeStruct((2 * slice_rows, width), BF),
        ],
    )(projected, expert_in, expert_out)
    mixed = lax.all_to_all(packed, "ctx", 0, 0, tiled=True)
    block = after(block, mixed)
    up, down = [shift(block, "ctx", 1)], [shift(block, "ctx", -1)]
    group = 2
    head_output = local(
        attend_kernel,
        jax.ShapeDtypeStruct((n, t * 3 // 2, 128), BF),
        [pltpu.VMEM((n * t, 128), BF)],
        grid=(n // group,),
        in_specs=[pl.BlockSpec((n, t * 9 // 2, 128), lambda i: (0, 0, 0))],
        out_specs=pl.BlockSpec((group, t * 3 // 2, 128), lambda i: (i, 0, 0)),
    )(mixed)
    back = lax.all_to_all(head_output, "ctx", 0, 0, tiled=True)
    part = cap // CHUNKS
    wide = (experts * part * 4 // 5, width * 5 // 4)
    stream, *sends = local(
        functools.partial(dispatch_kernel, experts, cap),
        [jax.ShapeDtypeStruct((t, width), F32)] + [jax.ShapeDtypeStruct(wide, BF)] * CHUNKS,
    )(back, residual_in[0], modulation_scale, modulation_shift, expert_choice[0].T)
    up[0], down[0] = after(up[0], *sends), after(down[0], *sends)
    for _ in range(n // 2 - 2):
        up.append(shift(up[-1], "ctx", 1))
        down.append(shift(down[-1], "ctx", -1))
    far_in = shift(up[-1][:slice_rows], "ctx", 1)
    far_out = shift(down[-1][slice_rows:], "ctx", -1)
    far = jnp.concatenate([far_in, far_out])
    weights = local(
        assemble_kernel, [jax.ShapeDtypeStruct((n * slice_rows, width), BF)] * 2
    )(block, *up, *down, far)
    arrived = [lax.all_to_all(x, "expert", 0, 0, tiled=True) for x in sends]
    sums = [expert_layer(x, weights) for x in arrived]
    returned = [lax.all_to_all(x, "expert", 0, 0, tiled=True) for x in sums]
    return local(
        functools.partial(combine_kernel, experts, cap),
        jax.ShapeDtypeStruct((1, t, width), BF),
    )(stream, expert_choice[0], gate_values[0], *returned)


def solution(mesh):
    return jax.shard_map(
        per_device,
        mesh=mesh,
        in_specs=(
            P(("dp", "expert"), None, "ctx", None),
            P(("dp", "expert"), "ctx", None),
            P(("dp", "expert"), None),
            P(("dp", "expert"), None),
            P(("dp", "expert"), "ctx", None),
            P(("dp", "expert"), "ctx", None),
            P("expert", ("dp", "ctx"), None),
            P("expert", ("dp", "ctx"), None),
        ),
        out_specs=P(("dp", "expert"), "ctx", None),
        check_vma=False,
    )
```

```python
import functools

import jax
import jax.numpy as jnp
from jax import lax
from jax.experimental import pallas as pl
from jax.experimental.pallas import tpu as pltpu
from jax.sharding import PartitionSpec as P

HD = 64
CHUNKS = 1
BF = jnp.bfloat16
F32 = jnp.float32
LIMIT = 48 * 1024 * 1024


def swap(x):
    return jnp.concatenate([x[:, HD:], x[:, :HD]], axis=1)


def low_lanes(rows):
    return lax.broadcasted_iota(jnp.int32, (rows, 2 * HD), 1) < HD


def join_kernel(in_ref, out_ref, w_ref):
    w_ref[: in_ref.shape[1], :] = in_ref[0]
    w_ref[in_ref.shape[1] :, :] = out_ref[0]


def pack_kernel(x_ref, o_ref):
    n = o_ref.shape[0]
    t = x_ref.shape[2]
    half = t // 2
    low, low_half = low_lanes(t), low_lanes(half)
    for j in range(n):
        for part in range(3):
            o_ref[j, part * t : (part + 1) * t, :] = x_ref[0, part, :, 128 * j : 128 * (j + 1)]
        at = 128 * (n + j // 2)
        q, k, v = (x_ref[0, part, :, at : at + 128] for part in range(3))
        if j % 2 == 0:
            o_ref[j, 3 * t : 4 * t, :] = jnp.where(low, q, swap(k))
            o_ref[j, 4 * t :, :] = jnp.where(low_half, v[:half], swap(v[half:]))
        else:
            o_ref[j, 3 * t : 4 * t, :] = jnp.where(low, swap(q), k)
            o_ref[j, 4 * t :, :] = jnp.where(low_half, swap(v[:half]), v[half:])


def attend_kernel(m_ref, o_ref, v2_ref):
    n, _, _ = m_ref.shape
    t = m_ref.shape[1] * 2 // 9
    half = t // 2
    group = o_ref.shape[0]
    step = pl.program_id(0)

    @pl.when(step == 0)
    def _():
        for z in range(n):
            block = m_ref[z, 4 * t :, :]
            v2_ref[z * t : z * t + half, :] = block
            v2_ref[z * t + half : (z + 1) * t, :] = swap(block)

    rows = group * t
    low = low_lanes(rows)
    mine = pl.ds(step * group, group)
    q01 = m_ref[mine, 0:t, :].reshape(rows, 128)
    q2 = swap(m_ref[mine, 3 * t : 4 * t, :].reshape(rows, 128))
    k01 = m_ref[:, t : 2 * t, :].reshape(n * t, 128)
    k2 = m_ref[:, 3 * t : 4 * t, :].reshape(n * t, 128)
    v01 = m_ref[:, 2 * t : 3 * t, :].reshape(n * t, 128)
    v2 = v2_ref[...]
    zero = jnp.zeros_like(q01)

    def head(q, k, v):
        scores = lax.dot_general(q, k, (((1,), (1,)), ((), ())), preferred_element_type=F32)
        scores = scores * HD ** (-0.5)
        probs = jnp.exp(scores - jnp.max(scores, axis=-1, keepdims=True))
        totals = jnp.sum(probs, axis=-1, keepdims=True)
        return jnp.dot(probs.astype(BF), v, preferred_element_type=F32) / totals

    a = head(jnp.where(low, q01, zero), k01, v01)
    b = head(jnp.where(low, zero, q01), k01, v01)
    c = head(jnp.where(low, zero, q2), k2, v2).astype(BF)
    pair = jnp.where(low, a, b).astype(BF)
    low_half = low_lanes(half)
    for g in range(group):
        o_ref[g, 0:t, :] = pair[g * t : (g + 1) * t]
        o_ref[g, t:, :] = jnp.where(
            low_half, c[g * t : g * t + half], swap(c[g * t + half : (g + 1) * t])
        )


def dispatch_kernel(experts, cap, b_ref, r_ref, scale_ref, shift_ref, choice_ref, s_ref, *sends):
    n = b_ref.shape[0]
    t, width = r_ref.shape
    half = t // 2
    low_half = low_lanes(half)
    tiles = [b_ref[j, 0:t, :] for j in range(n)]
    for m in range(n // 2):
        even, odd = b_ref[2 * m, t:, :], b_ref[2 * m + 1, t:, :]
        top = jnp.where(low_half, even, swap(odd))
        bottom = jnp.where(low_half, swap(even), odd)
        tiles.append(jnp.concatenate([top, bottom], axis=0))
    attended = jnp.concatenate(tiles, axis=1)
    stream = r_ref[...].astype(F32) + attended.astype(F32)
    s_ref[...] = stream
    mean_square = jnp.mean(stream * stream, axis=-1, keepdims=True)
    normed = (
        stream / jnp.sqrt(mean_square + 1e-06) * (1.0 + scale_ref[...]) + shift_ref[...]
    ).astype(BF)
    choices = choice_ref[...]
    expert_at = lax.broadcasted_iota(jnp.int32, (experts, t), 0)
    first, second = expert_at == choices[0:1], expert_at == choices[1:2]
    earlier = lax.broadcasted_iota(jnp.int32, (t, t), 0) < lax.broadcasted_iota(
        jnp.int32, (t, t), 1
    )
    before = jnp.dot(
        (first | second).astype(F32).astype(BF),
        earlier.astype(F32).astype(BF),
        preferred_element_type=F32,
    ).astype(jnp.int32)
    keys = [
        choices[k : k + 1] * 32 + jnp.sum(jnp.where(named, before, 0), axis=0, keepdims=True)
        for k, named in enumerate((first, second))
    ]
    part = cap // len(sends)
    main, extra = part * 4 // 5, part // 5
    rows = experts * main
    at = lax.broadcasted_iota(jnp.int32, (rows, 1), 0)
    quarter = width // 4
    for c, send in enumerate(sends):
        main_key = at // main * 32 + c * part + at % main
        pick = ((main_key == keys[0]) | (main_key == keys[1])).astype(F32).astype(BF)
        send[:, :width] = jnp.dot(pick, normed, preferred_element_type=F32).astype(BF)
        extra_key = at // main * 32 + c * part + main + at % main // 4
        matches = (extra_key == keys[0]) | (extra_key == keys[1])
        total = jnp.zeros((rows, quarter), F32)
        for q in range(4):
            pick = (matches & (at % 4 == q)).astype(F32).astype(BF)
            total += jnp.dot(
                pick, normed[:, q * quarter : (q + 1) * quarter], preferred_element_type=F32
            )
        send[:, width:] = total.astype(BF)


def assemble_kernel(*refs):
    far_in, far_out, *blocks, in_ref, out_ref = refs
    rows = far_in.shape[0]
    in_ref[len(blocks) * rows :, :] = far_in[...]
    out_ref[len(blocks) * rows :, :] = far_out[...]
    for i, block in enumerate(blocks):
        in_ref[i * rows : (i + 1) * rows, :] = block[:rows, :]
        out_ref[i * rows : (i + 1) * rows, :] = block[rows:, :]


def expert_kernel(pieces, in_ref, out_ref, *refs):
    x_refs, plus, y_refs, rows_ref = refs[:pieces], refs[pieces : -pieces - 1], refs[-pieces - 1 : -1], refs[-1]
    rows = x_refs[0].shape[0]
    width = in_ref.shape[1]
    quarter = width // 4
    extras = rows // 4
    every = rows + extras
    row_at = lax.broadcasted_iota(jnp.int32, (extras, rows), 0)
    source = lax.broadcasted_iota(jnp.int32, (extras, rows), 1)
    picks = [(source == 4 * row_at + q).astype(F32).astype(BF) for q in range(4)]
    for p, x_ref in enumerate(x_refs):
        base = p * every
        rows_ref[base : base + rows, :] = x_ref[:, :width]
        packed = x_ref[:, width:]
        for q in range(4):
            rows_ref[base + rows : base + every, q * quarter : (q + 1) * quarter] = jnp.dot(
                picks[q], packed, preferred_element_type=F32
            ).astype(BF)
    pre_act = lax.dot_general(
        rows_ref[...], in_ref[...], (((1,), (1,)), ((), ())), preferred_element_type=F32
    )
    hidden = jax.nn.gelu(pre_act, approximate=True).astype(BF)
    partial = jnp.dot(hidden, out_ref[...], preferred_element_type=F32).astype(BF)
    to = lax.broadcasted_iota(jnp.int32, (rows, extras), 0)
    origin = lax.broadcasted_iota(jnp.int32, (rows, extras), 1)
    picks = [(to == 4 * origin + q).astype(F32).astype(BF) for q in range(4)]
    for p, y_ref in enumerate(y_refs):
        base = p * every
        main = partial[base : base + rows]
        total = jnp.zeros((rows, quarter), F32)
        for q in range(4):
            total += jnp.dot(
                picks[q],
                partial[base + rows : base + every, q * quarter : (q + 1) * quarter],
                preferred_element_type=F32,
            )
        total = total.astype(BF)
        if plus:
            main = add(main, plus[p][:, :width])
            total = add(total, plus[p][:, width:])
        y_ref[:, :width] = main
        y_ref[:, width:] = total


def combine_kernel(experts, cap, s_ref, choice_ref, gate_ref, *refs):
    returned, o_ref = refs[:-1], refs[-1]
    t, width = s_ref.shape
    choices = choice_ref[...]
    expert_at = lax.broadcasted_iota(jnp.int32, (t, 128), 1)
    first, second = expert_at == choices[:, 0:1], expert_at == choices[:, 1:2]
    earlier = lax.broadcasted_iota(jnp.int32, (t, t), 1) < lax.broadcasted_iota(
        jnp.int32, (t, t), 0
    )
    before = jnp.dot(
        earlier.astype(F32).astype(BF),
        (first | second).astype(F32).astype(BF),
        preferred_element_type=F32,
    ).astype(jnp.int32)
    keys = jnp.concatenate(
        [
            choices[:, k : k + 1] * 32
            + jnp.sum(jnp.where(named, before, 0), axis=1, keepdims=True)
            for k, named in enumerate((first, second))
        ],
        axis=0,
    )
    part = cap // len(returned)
    main, extra = part * 4 // 5, part // 5
    rows = experts * main
    at = lax.broadcasted_iota(jnp.int32, (1, rows), 1)
    quarter = width // 4
    picked = jnp.zeros((2 * t, width), F32)
    for c, back in enumerate(returned):
        main_key = at // main * 32 + c * part + at % main
        pick = (main_key == keys).astype(F32).astype(BF)
        picked += jnp.dot(pick, back[:, :width], preferred_element_type=F32)
        extra_key = at // main * 32 + c * part + main + at % main // 4
        parts = []
        for q in range(4):
            pick = ((extra_key == keys) & (at % 4 == q)).astype(F32).astype(BF)
            parts.append(jnp.dot(pick, back[:, width:], preferred_element_type=F32))
        picked += jnp.concatenate(parts, axis=1)
    gates = gate_ref[...]
    mixture = gates[:, 0:1] * picked[:t] + gates[:, 1:2] * picked[t:]
    o_ref[0] = (s_ref[...] + mixture).astype(BF)


def local(kernel, out_shape, scratch=(), **more):
    return pl.pallas_call(
        kernel,
        out_shape=out_shape,
        scratch_shapes=scratch,
        compiler_params=pltpu.CompilerParams(vmem_limit_bytes=LIMIT),
        **more,
    )


def run_experts(pieces, weight_in, weight_out, plus=()):
    rows, wide = pieces[0].shape
    hidden, width = weight_in.shape
    work = len(pieces) * rows * 5 // 4
    return local(
        functools.partial(expert_kernel, len(pieces)),
        [jax.ShapeDtypeStruct((rows, wide), BF)] * len(pieces),
        [pltpu.VMEM((work, width), BF)],
        cost_estimate=pl.CostEstimate(
            flops=4 * work * hidden * width,
            bytes_accessed=4 * hidden * width + 4 * len(pieces) * rows * wide,
            transcendentals=work * hidden,
        ),
    )(weight_in, weight_out, *pieces, *plus)


def add(*parts):
    return sum(p.astype(F32) for p in parts).astype(BF)


def shift(x, axis, by):
    n = lax.axis_size(axis)
    return lax.ppermute(x, axis, [(i, (i + by) % n) for i in range(n)])


def after(x, *others):
    return lax.optimization_barrier((x, *others))[0]


def ring_in(x):
    half = x.shape[0] // 2
    a, b = x[:half], x[half:]
    left_a, right_b = shift(a, "dp", 1), shift(b, "dp", -1)
    left_b, right_a = shift(b, "dp", 1), shift(a, "dp", -1)
    across_a, across_b = shift(left_a, "dp", 1), shift(right_b, "dp", -1)
    return (a, b), (left_a, left_b, right_a, right_b), (across_a, across_b)


def expert_layer(own, near, across, weights):
    to_left_a, to_left_b, to_right_a, to_right_b = run_experts(near, *weights)
    got_a, got_b = shift(to_left_a, "dp", -1), shift(to_right_b, "dp", 1)
    across = after(across, to_left_a)
    to_across_a, to_across_b = run_experts(across, *weights)
    via_a, via_b = shift(to_across_a, "dp", 1), shift(to_across_b, "dp", -1)
    own = after(own, to_across_a)
    own_a, own_b = run_experts(own, *weights, plus=(got_a, got_b))
    sum_a = shift(add(to_right_a, via_a), "dp", 1)
    sum_b = shift(add(to_left_b, via_b), "dp", -1)
    return jnp.concatenate([add(own_a, sum_a), add(own_b, sum_b)])


def per_device(
    projected,
    residual_in,
    modulation_scale,
    modulation_shift,
    expert_choice,
    gate_values,
    expert_in,
    expert_out,
):
    _, _, t, width = projected.shape
    n = lax.axis_size("ctx")
    experts = lax.axis_size("expert")
    cap = 5 * t * 2 // (4 * experts)
    slice_rows = expert_in.shape[1]
    packed = local(pack_kernel, jax.ShapeDtypeStruct((n, t * 9 // 2, 128), BF))(projected)
    block = local(join_kernel, jax.ShapeDtypeStruct((2 * slice_rows, width), BF))(
        expert_in, expert_out
    )
    mixed = lax.all_to_all(packed, "ctx", 0, 0, tiled=True)
    block = after(block, mixed)
    up, down = [shift(block, "ctx", 1)], [shift(block, "ctx", -1)]
    group = 2
    head_output = local(
        attend_kernel,
        jax.ShapeDtypeStruct((n, t * 3 // 2, 128), BF),
        [pltpu.VMEM((n * t, 128), BF)],
        grid=(n // group,),
        in_specs=[pl.BlockSpec((n, t * 9 // 2, 128), lambda i: (0, 0, 0))],
        out_specs=pl.BlockSpec((group, t * 3 // 2, 128), lambda i: (i, 0, 0)),
    )(mixed)
    back = lax.all_to_all(head_output, "ctx", 0, 0, tiled=True)
    back, up[0], down[0] = lax.optimization_barrier((back, up[0], down[0]))
    part = cap // CHUNKS
    wide = (experts * part * 4 // 5, width * 5 // 4)
    stream, *sends = local(
        functools.partial(dispatch_kernel, experts, cap),
        [jax.ShapeDtypeStruct((t, width), F32)] + [jax.ShapeDtypeStruct(wide, BF)] * CHUNKS,
    )(back, residual_in[0], modulation_scale, modulation_shift, expert_choice[0].T)
    up[0], down[0] = after(up[0], *sends), after(down[0], *sends)
    arrived = [lax.all_to_all(x, "expert", 0, 0, tiled=True) for x in sends]
    for _ in range(n // 2 - 2):
        up.append(shift(up[-1], "ctx", 1))
        down.append(shift(down[-1], "ctx", -1))
    rings = [ring_in(x) for x in arrived]
    first = rings[0][0]
    up[-1], down[-1] = after((up[-1], down[-1]), first)
    far_in = shift(up[-1][:slice_rows], "ctx", 1)
    far_out = shift(down[-1][slice_rows:], "ctx", -1)
    weights = local(
        assemble_kernel, [jax.ShapeDtypeStruct((n * slice_rows, width), BF)] * 2
    )(far_in, far_out, block, *up, *down)
    sums = [expert_layer(*ring, weights) for ring in rings]
    returned = [lax.all_to_all(x, "expert", 0, 0, tiled=True) for x in sums]
    return local(
        functools.partial(combine_kernel, experts, cap),
        jax.ShapeDtypeStruct((1, t, width), BF),
    )(stream, expert_choice[0], gate_values[0], *returned)


def solution(mesh):
    return jax.shard_map(
        per_device,
        mesh=mesh,
        in_specs=(
            P(("dp", "expert"), None, "ctx", None),
            P(("dp", "expert"), "ctx", None),
            P(("dp", "expert"), None),
            P(("dp", "expert"), None),
            P(("dp", "expert"), "ctx", None),
            P(("dp", "expert"), "ctx", None),
            P("expert", ("dp", "ctx"), None),
            P("expert", ("dp", "ctx"), None),
        ),
        out_specs=P(("dp", "expert"), "ctx", None),
        check_vma=False,
    )
```

```python
import functools

import jax
import jax.numpy as jnp
from jax import lax
from jax.experimental import pallas as pl
from jax.experimental.pallas import tpu as pltpu
from jax.sharding import PartitionSpec as P

HD = 64
CHUNKS = 2
BF = jnp.bfloat16
F32 = jnp.float32
LIMIT = 24 * 1024 * 1024


def swap(x):
    return jnp.concatenate([x[:, HD:], x[:, :HD]], axis=1)


def low_lanes(rows):
    return lax.broadcasted_iota(jnp.int32, (rows, 2 * HD), 1) < HD


def join_kernel(in_ref, out_ref, w_ref):
    w_ref[: in_ref.shape[1], :] = in_ref[0]
    w_ref[in_ref.shape[1] :, :] = out_ref[0]


def pack_kernel(x_ref, o_ref):
    n = o_ref.shape[0]
    t = x_ref.shape[2]
    half = t // 2
    low, low_half = low_lanes(t), low_lanes(half)
    for j in range(n):
        for part in range(3):
            o_ref[j, part * t : (part + 1) * t, :] = x_ref[0, part, :, 128 * j : 128 * (j + 1)]
        at = 128 * (n + j // 2)
        q, k, v = (x_ref[0, part, :, at : at + 128] for part in range(3))
        if j % 2 == 0:
            o_ref[j, 3 * t : 4 * t, :] = jnp.where(low, q, swap(k))
            o_ref[j, 4 * t :, :] = jnp.where(low_half, v[:half], swap(v[half:]))
        else:
            o_ref[j, 3 * t : 4 * t, :] = jnp.where(low, swap(q), k)
            o_ref[j, 4 * t :, :] = jnp.where(low_half, swap(v[:half]), v[half:])


def attend_kernel(m_ref, o_ref, v2_ref):
    n, _, _ = m_ref.shape
    t = m_ref.shape[1] * 2 // 9
    half = t // 2
    group = o_ref.shape[0]
    step = pl.program_id(0)

    @pl.when(step == 0)
    def _():
        for z in range(n):
            block = m_ref[z, 4 * t :, :]
            v2_ref[z * t : z * t + half, :] = block
            v2_ref[z * t + half : (z + 1) * t, :] = swap(block)

    rows = group * t
    low = low_lanes(rows)
    mine = pl.ds(step * group, group)
    scaling = jnp.asarray(HD ** (-0.5), BF)
    q01 = m_ref[mine, 0:t, :].reshape(rows, 128) * scaling
    q2 = swap(m_ref[mine, 3 * t : 4 * t, :].reshape(rows, 128)) * scaling
    k01 = m_ref[:, t : 2 * t, :].reshape(n * t, 128)
    k2 = m_ref[:, 3 * t : 4 * t, :].reshape(n * t, 128)
    v01 = m_ref[:, 2 * t : 3 * t, :].reshape(n * t, 128)
    v2 = v2_ref[...]
    zero = jnp.zeros_like(q01)

    def head(q, k, v):
        scores = lax.dot_general(q, k, (((1,), (1,)), ((), ())), preferred_element_type=F32)
        probs = jnp.exp(scores - jnp.max(scores, axis=-1, keepdims=True))
        totals = jnp.sum(probs, axis=-1, keepdims=True)
        return jnp.dot(probs.astype(BF), v, preferred_element_type=F32) / totals

    a = head(jnp.where(low, q01, zero), k01, v01)
    b = head(jnp.where(low, zero, q01), k01, v01)
    c = head(jnp.where(low, zero, q2), k2, v2).astype(BF)
    pair = jnp.where(low, a, b).astype(BF)
    low_half = low_lanes(half)
    for g in range(group):
        o_ref[g, 0:t, :] = pair[g * t : (g + 1) * t]
        o_ref[g, t:, :] = jnp.where(
            low_half, c[g * t : g * t + half], swap(c[g * t + half : (g + 1) * t])
        )


def dispatch_kernel(experts, cap, b_ref, r_ref, scale_ref, shift_ref, choice_ref, s_ref, *sends):
    n = b_ref.shape[0]
    t, width = r_ref.shape
    half = t // 2
    low_half = low_lanes(half)
    tiles = [b_ref[j, 0:t, :] for j in range(n)]
    for m in range(n // 2):
        even, odd = b_ref[2 * m, t:, :], b_ref[2 * m + 1, t:, :]
        top = jnp.where(low_half, even, swap(odd))
        bottom = jnp.where(low_half, swap(even), odd)
        tiles.append(jnp.concatenate([top, bottom], axis=0))
    attended = jnp.concatenate(tiles, axis=1)
    stream = r_ref[...].astype(F32) + attended.astype(F32)
    s_ref[...] = stream
    mean_square = jnp.mean(stream * stream, axis=-1, keepdims=True)
    normed = (
        stream / jnp.sqrt(mean_square + 1e-06) * (1.0 + scale_ref[...]) + shift_ref[...]
    ).astype(BF)
    choices = choice_ref[...]
    expert_at = lax.broadcasted_iota(jnp.int32, (experts, t), 0)
    first, second = expert_at == choices[0:1], expert_at == choices[1:2]
    earlier = lax.broadcasted_iota(jnp.int32, (t, t), 0) < lax.broadcasted_iota(
        jnp.int32, (t, t), 1
    )
    before = jnp.dot(
        (first | second).astype(F32).astype(BF),
        earlier.astype(F32).astype(BF),
        preferred_element_type=F32,
    ).astype(jnp.int32)
    keys = [
        choices[k : k + 1] * 32 + jnp.sum(jnp.where(named, before, 0), axis=0, keepdims=True)
        for k, named in enumerate((first, second))
    ]
    part = cap // len(sends)
    main, extra = part * 4 // 5, part // 5
    rows = experts * main
    at = lax.broadcasted_iota(jnp.int32, (rows, 1), 0)
    quarter = width // 4
    for c, send in enumerate(sends):
        main_key = at // main * 32 + c * part + at % main
        pick = ((main_key == keys[0]) | (main_key == keys[1])).astype(F32).astype(BF)
        send[:, :width] = jnp.dot(pick, normed, preferred_element_type=F32).astype(BF)
        extra_key = at // main * 32 + c * part + main + at % main // 4
        matches = (extra_key == keys[0]) | (extra_key == keys[1])
        total = jnp.zeros((rows, quarter), F32)
        for q in range(4):
            pick = (matches & (at % 4 == q)).astype(F32).astype(BF)
            total += jnp.dot(
                pick, normed[:, q * quarter : (q + 1) * quarter], preferred_element_type=F32
            )
        send[:, width:] = total.astype(BF)


def assemble_kernel(*refs):
    far_in, far_out, *blocks, in_ref, out_ref = refs
    rows = far_in.shape[0]
    in_ref[len(blocks) * rows :, :] = far_in[...]
    out_ref[len(blocks) * rows :, :] = far_out[...]
    for i, block in enumerate(blocks):
        in_ref[i * rows : (i + 1) * rows, :] = block[:rows, :]
        out_ref[i * rows : (i + 1) * rows, :] = block[rows:, :]


def expert_kernel(pieces, in_ref, out_ref, *refs):
    x_refs, plus, y_refs, rows_ref = refs[:pieces], refs[pieces : -pieces - 1], refs[-pieces - 1 : -1], refs[-1]
    rows = x_refs[0].shape[0]
    width = in_ref.shape[1]
    quarter = width // 4
    extras = rows // 4
    every = rows + extras
    row_at = lax.broadcasted_iota(jnp.int32, (rows, rows), 0)
    source = lax.broadcasted_iota(jnp.int32, (rows, rows), 1)
    pick = (source == 4 * (row_at % extras) + row_at // extras).astype(F32).astype(BF)
    for p, x_ref in enumerate(x_refs):
        base = p * every
        rows_ref[base : base + rows, :] = x_ref[:, :width]
        quarters = jnp.dot(pick, x_ref[:, width:], preferred_element_type=F32).astype(BF)
        for q in range(4):
            rows_ref[base + rows : base + every, q * quarter : (q + 1) * quarter] = quarters[
                q * extras : (q + 1) * extras
            ]
    pre_act = lax.dot_general(
        rows_ref[...], in_ref[...], (((1,), (1,)), ((), ())), preferred_element_type=F32
    )
    hidden = jax.nn.gelu(pre_act, approximate=True).astype(BF)
    partial = jnp.dot(hidden, out_ref[...], preferred_element_type=F32).astype(BF)
    pack = (row_at == 4 * (source % extras) + source // extras).astype(F32).astype(BF)
    for p, y_ref in enumerate(y_refs):
        base = p * every
        main = partial[base : base + rows]
        last = partial[base + rows : base + every]
        quarters = jnp.concatenate(
            [last[:, q * quarter : (q + 1) * quarter] for q in range(4)], axis=0
        )
        total = jnp.dot(pack, quarters, preferred_element_type=F32).astype(BF)
        if plus:
            main = add(main, plus[p][:, :width])
            total = add(total, plus[p][:, width:])
        y_ref[:, :width] = main
        y_ref[:, width:] = total


def combine_kernel(experts, cap, s_ref, choice_ref, gate_ref, *refs):
    returned, o_ref = refs[:-1], refs[-1]
    t, width = s_ref.shape
    choices = choice_ref[...]
    expert_at = lax.broadcasted_iota(jnp.int32, (t, 128), 1)
    first, second = expert_at == choices[:, 0:1], expert_at == choices[:, 1:2]
    earlier = lax.broadcasted_iota(jnp.int32, (t, t), 1) < lax.broadcasted_iota(
        jnp.int32, (t, t), 0
    )
    before = jnp.dot(
        earlier.astype(F32).astype(BF),
        (first | second).astype(F32).astype(BF),
        preferred_element_type=F32,
    ).astype(jnp.int32)
    keys = jnp.concatenate(
        [
            choices[:, k : k + 1] * 32
            + jnp.sum(jnp.where(named, before, 0), axis=1, keepdims=True)
            for k, named in enumerate((first, second))
        ],
        axis=0,
    )
    part = cap // len(returned)
    main, extra = part * 4 // 5, part // 5
    rows = experts * main
    at = lax.broadcasted_iota(jnp.int32, (1, rows), 1)
    quarter = width // 4
    picked = jnp.zeros((2 * t, width), F32)
    for c, back in enumerate(returned):
        main_key = at // main * 32 + c * part + at % main
        pick = (main_key == keys).astype(F32).astype(BF)
        picked += jnp.dot(pick, back[:, :width], preferred_element_type=F32)
        extra_key = at // main * 32 + c * part + main + at % main // 4
        parts = []
        for q in range(4):
            pick = ((extra_key == keys) & (at % 4 == q)).astype(F32).astype(BF)
            parts.append(jnp.dot(pick, back[:, width:], preferred_element_type=F32))
        picked += jnp.concatenate(parts, axis=1)
    gates = gate_ref[...]
    mixture = gates[:, 0:1] * picked[:t] + gates[:, 1:2] * picked[t:]
    o_ref[0] = (s_ref[...] + mixture).astype(BF)


def local(kernel, out_shape, scratch=(), **more):
    return pl.pallas_call(
        kernel,
        out_shape=out_shape,
        scratch_shapes=scratch,
        compiler_params=pltpu.CompilerParams(vmem_limit_bytes=LIMIT),
        **more,
    )


def run_experts(pieces, weight_in, weight_out, plus=()):
    rows, wide = pieces[0].shape
    hidden, width = weight_in.shape
    work = len(pieces) * rows * 5 // 4
    return local(
        functools.partial(expert_kernel, len(pieces)),
        [jax.ShapeDtypeStruct((rows, wide), BF)] * len(pieces),
        [pltpu.VMEM((work, width), BF)],
        cost_estimate=pl.CostEstimate(
            flops=4 * work * hidden * width,
            bytes_accessed=4 * hidden * width + 4 * len(pieces) * rows * wide,
            transcendentals=work * hidden,
        ),
    )(weight_in, weight_out, *pieces, *plus)


def add(*parts):
    return sum(p.astype(F32) for p in parts).astype(BF)


def shift(x, axis, by):
    n = lax.axis_size(axis)
    return lax.ppermute(x, axis, [(i, (i + by) % n) for i in range(n)])


def after(x, *others):
    return lax.optimization_barrier((x, *others))[0]


def ring_in(a, b):
    left_a, right_a = shift(a, "dp", 1), shift(a, "dp", -1)
    across_a = shift(left_a, "dp", 1)
    b = after(b, left_a, right_a)
    left_b, right_b = shift(b, "dp", 1), shift(b, "dp", -1)
    across_b = shift(right_b, "dp", -1)
    return (a, b), (left_a, left_b, right_a, right_b), (across_a, across_b)


def expert_layer(own, near, across, weights):
    to_left_a, to_left_b, to_right_a, to_right_b = run_experts(near, *weights)
    got_a, got_b = shift(to_left_a, "dp", -1), shift(to_right_b, "dp", 1)
    across = after(across, to_left_a)
    to_across_a, to_across_b = run_experts(across, *weights)
    via_a, via_b = shift(to_across_a, "dp", 1), shift(to_across_b, "dp", -1)
    via_a, via_b = add(to_right_a, via_a), add(to_left_b, via_b)
    sum_a, sum_b = shift(via_a, "dp", 1), shift(via_b, "dp", -1)
    own = after(own, via_a, via_b)
    own_a, own_b = run_experts(own, *weights, plus=(got_a, got_b))
    return add(own_a, sum_a), add(own_b, sum_b)


def per_device(
    projected,
    residual_in,
    modulation_scale,
    modulation_shift,
    expert_choice,
    gate_values,
    expert_in,
    expert_out,
):
    _, _, t, width = projected.shape
    n = lax.axis_size("ctx")
    experts = lax.axis_size("expert")
    cap = 5 * t * 2 // (4 * experts)
    slice_rows = expert_in.shape[1]
    packed = local(pack_kernel, jax.ShapeDtypeStruct((n, t * 9 // 2, 128), BF))(projected)
    block = local(join_kernel, jax.ShapeDtypeStruct((2 * slice_rows, width), BF))(
        expert_in, expert_out
    )
    mixed = lax.all_to_all(packed, "ctx", 0, 0, tiled=True)
    group = 2
    head_output = local(
        attend_kernel,
        jax.ShapeDtypeStruct((n, t * 3 // 2, 128), BF),
        [pltpu.VMEM((n * t, 128), BF)],
        grid=(n // group,),
        in_specs=[pl.BlockSpec((n, t * 9 // 2, 128), lambda i: (0, 0, 0))],
        out_specs=pl.BlockSpec((group, t * 3 // 2, 128), lambda i: (i, 0, 0)),
    )(mixed)
    back = lax.all_to_all(head_output, "ctx", 0, 0, tiled=True)
    part = cap // CHUNKS
    wide = (experts * part * 4 // 5, width * 5 // 4)
    stream, *sends = local(
        functools.partial(dispatch_kernel, experts, cap),
        [jax.ShapeDtypeStruct((t, width), F32)] + [jax.ShapeDtypeStruct(wide, BF)] * CHUNKS,
    )(back, residual_in[0], modulation_scale, modulation_shift, expert_choice[0].T)
    block = after(block, *sends)
    up, down = [shift(block, "ctx", 1)], [shift(block, "ctx", -1)]
    arrived = [lax.all_to_all(x, "expert", 0, 0, tiled=True) for x in sends]
    for _ in range(n // 2 - 2):
        up.append(shift(up[-1], "ctx", 1))
        down.append(shift(down[-1], "ctx", -1))
    ring = ring_in(*arrived)
    far_in = shift(up[-1][:slice_rows], "ctx", 1)
    far_out = shift(down[-1][slice_rows:], "ctx", -1)
    weights = local(
        assemble_kernel, [jax.ShapeDtypeStruct((n * slice_rows, width), BF)] * 2
    )(far_in, far_out, block, *up, *down)
    sums = expert_layer(*ring, weights)
    returned = [lax.all_to_all(x, "expert", 0, 0, tiled=True) for x in sums]
    return local(
        functools.partial(combine_kernel, experts, cap),
        jax.ShapeDtypeStruct((1, t, width), BF),
    )(stream, expert_choice[0], gate_values[0], *returned)


def solution(mesh):
    return jax.shard_map(
        per_device,
        mesh=mesh,
        in_specs=(
            P(("dp", "expert"), None, "ctx", None),
            P(("dp", "expert"), "ctx", None),
            P(("dp", "expert"), None),
            P(("dp", "expert"), None),
            P(("dp", "expert"), "ctx", None),
            P(("dp", "expert"), "ctx", None),
            P("expert", ("dp", "ctx"), None),
            P("expert", ("dp", "ctx"), None),
        ),
        out_specs=P(("dp", "expert"), "ctx", None),
        check_vma=False,
    )
```

```python
import functools

import jax
import jax.numpy as jnp
from jax import lax
from jax.experimental import pallas as pl
from jax.experimental.pallas import tpu as pltpu
from jax.sharding import PartitionSpec as P

HD = 64
CHUNKS = 1
BF = jnp.bfloat16
F32 = jnp.float32
LIMIT = 24 * 1024 * 1024


def swap(x):
    return jnp.concatenate([x[:, HD:], x[:, :HD]], axis=1)


def low_lanes(rows):
    return lax.broadcasted_iota(jnp.int32, (rows, 2 * HD), 1) < HD


def join_kernel(in_ref, out_ref, w_ref):
    w_ref[: in_ref.shape[1], :] = in_ref[0]
    w_ref[in_ref.shape[1] :, :] = out_ref[0]


def pack_kernel(x_ref, o_ref):
    n = o_ref.shape[0]
    t = x_ref.shape[2]
    half = t // 2
    low, low_half = low_lanes(t), low_lanes(half)
    for j in range(n):
        for part in range(3):
            o_ref[j, part * t : (part + 1) * t, :] = x_ref[0, part, :, 128 * j : 128 * (j + 1)]
        at = 128 * (n + j // 2)
        q, k, v = (x_ref[0, part, :, at : at + 128] for part in range(3))
        if j % 2 == 0:
            o_ref[j, 3 * t : 4 * t, :] = jnp.where(low, q, swap(k))
            o_ref[j, 4 * t :, :] = jnp.where(low_half, v[:half], swap(v[half:]))
        else:
            o_ref[j, 3 * t : 4 * t, :] = jnp.where(low, swap(q), k)
            o_ref[j, 4 * t :, :] = jnp.where(low_half, swap(v[:half]), v[half:])


def attend_kernel(m_ref, o_ref, v2_ref):
    n, _, _ = m_ref.shape
    t = m_ref.shape[1] * 2 // 9
    half = t // 2
    group = o_ref.shape[0]
    step = pl.program_id(0)

    @pl.when(step == 0)
    def _():
        for z in range(n):
            block = m_ref[z, 4 * t :, :]
            v2_ref[z * t : z * t + half, :] = block
            v2_ref[z * t + half : (z + 1) * t, :] = swap(block)

    rows = group * t
    low = low_lanes(rows)
    mine = pl.ds(step * group, group)
    scaling = jnp.asarray(HD ** (-0.5), BF)
    q01 = m_ref[mine, 0:t, :].reshape(rows, 128) * scaling
    q2 = swap(m_ref[mine, 3 * t : 4 * t, :].reshape(rows, 128)) * scaling
    k01 = m_ref[:, t : 2 * t, :].reshape(n * t, 128)
    k2 = m_ref[:, 3 * t : 4 * t, :].reshape(n * t, 128)
    v01 = m_ref[:, 2 * t : 3 * t, :].reshape(n * t, 128)
    v2 = v2_ref[...]
    zero = jnp.zeros_like(q01)

    def head(q, k, v):
        scores = lax.dot_general(q, k, (((1,), (1,)), ((), ())), preferred_element_type=F32)
        probs = jnp.exp(scores - jnp.max(scores, axis=-1, keepdims=True))
        totals = jnp.sum(probs, axis=-1, keepdims=True)
        return jnp.dot(probs.astype(BF), v, preferred_element_type=F32) / totals

    a = head(jnp.where(low, q01, zero), k01, v01)
    b = head(jnp.where(low, zero, q01), k01, v01)
    c = head(jnp.where(low, zero, q2), k2, v2).astype(BF)
    pair = jnp.where(low, a, b).astype(BF)
    low_half = low_lanes(half)
    for g in range(group):
        o_ref[g, 0:t, :] = pair[g * t : (g + 1) * t]
        o_ref[g, t:, :] = jnp.where(
            low_half, c[g * t : g * t + half], swap(c[g * t + half : (g + 1) * t])
        )


def dispatch_kernel(experts, cap, b_ref, r_ref, scale_ref, shift_ref, choice_ref, s_ref, *sends):
    n = b_ref.shape[0]
    t, width = r_ref.shape
    half = t // 2
    low_half = low_lanes(half)
    tiles = [b_ref[j, 0:t, :] for j in range(n)]
    for m in range(n // 2):
        even, odd = b_ref[2 * m, t:, :], b_ref[2 * m + 1, t:, :]
        top = jnp.where(low_half, even, swap(odd))
        bottom = jnp.where(low_half, swap(even), odd)
        tiles.append(jnp.concatenate([top, bottom], axis=0))
    attended = jnp.concatenate(tiles, axis=1)
    stream = r_ref[...].astype(F32) + attended.astype(F32)
    s_ref[...] = stream
    mean_square = jnp.mean(stream * stream, axis=-1, keepdims=True)
    normed = (
        stream / jnp.sqrt(mean_square + 1e-06) * (1.0 + scale_ref[...]) + shift_ref[...]
    ).astype(BF)
    choices = choice_ref[...]
    expert_at = lax.broadcasted_iota(jnp.int32, (experts, t), 0)
    first, second = expert_at == choices[0:1], expert_at == choices[1:2]
    earlier = lax.broadcasted_iota(jnp.int32, (t, t), 0) < lax.broadcasted_iota(
        jnp.int32, (t, t), 1
    )
    before = jnp.dot(
        (first | second).astype(F32).astype(BF),
        earlier.astype(F32).astype(BF),
        preferred_element_type=F32,
    ).astype(jnp.int32)
    keys = [
        choices[k : k + 1] * 32 + jnp.sum(jnp.where(named, before, 0), axis=0, keepdims=True)
        for k, named in enumerate((first, second))
    ]
    part = cap // len(sends)
    main, extra = part * 4 // 5, part // 5
    rows = experts * main
    at = lax.broadcasted_iota(jnp.int32, (rows, 1), 0)
    quarter = width // 4
    for c, send in enumerate(sends):
        main_key = at // main * 32 + c * part + at % main
        pick = ((main_key == keys[0]) | (main_key == keys[1])).astype(F32).astype(BF)
        send[:, :width] = jnp.dot(pick, normed, preferred_element_type=F32).astype(BF)
        extra_key = at // main * 32 + c * part + main + at % main // 4
        matches = (extra_key == keys[0]) | (extra_key == keys[1])
        total = jnp.zeros((rows, quarter), F32)
        for q in range(4):
            pick = (matches & (at % 4 == q)).astype(F32).astype(BF)
            total += jnp.dot(
                pick, normed[:, q * quarter : (q + 1) * quarter], preferred_element_type=F32
            )
        send[:, width:] = total.astype(BF)


def assemble_kernel(*refs):
    *blocks, in_ref, out_ref = refs
    rows = in_ref.shape[0] // len(blocks)
    for i, block in enumerate(blocks):
        in_ref[i * rows : (i + 1) * rows, :] = block[:rows, :]
        out_ref[i * rows : (i + 1) * rows, :] = block[rows:, :]


def expert_kernel(pieces, in_ref, out_ref, *refs):
    x_refs, y_refs, rows_ref = refs[:pieces], refs[pieces:-1], refs[-1]
    rows = x_refs[0].shape[0]
    width = in_ref.shape[1]
    quarter = width // 4
    extras = rows // 4
    every = rows + extras
    row_at = lax.broadcasted_iota(jnp.int32, (rows, rows), 0)
    source = lax.broadcasted_iota(jnp.int32, (rows, rows), 1)
    pick = (source == 4 * (row_at % extras) + row_at // extras).astype(F32).astype(BF)
    for p, x_ref in enumerate(x_refs):
        base = p * every
        rows_ref[base : base + rows, :] = x_ref[:, :width]
        quarters = jnp.dot(pick, x_ref[:, width:], preferred_element_type=F32).astype(BF)
        for q in range(4):
            rows_ref[base + rows : base + every, q * quarter : (q + 1) * quarter] = quarters[
                q * extras : (q + 1) * extras
            ]
    pre_act = lax.dot_general(
        rows_ref[...], in_ref[...], (((1,), (1,)), ((), ())), preferred_element_type=F32
    )
    hidden = jax.nn.gelu(pre_act, approximate=True).astype(BF)
    partial = jnp.dot(hidden, out_ref[...], preferred_element_type=F32).astype(BF)
    pack = (row_at == 4 * (source % extras) + source // extras).astype(F32).astype(BF)
    for p, y_ref in enumerate(y_refs):
        base = p * every
        main = partial[base : base + rows]
        last = partial[base + rows : base + every]
        quarters = jnp.concatenate(
            [last[:, q * quarter : (q + 1) * quarter] for q in range(4)], axis=0
        )
        total = jnp.dot(pack, quarters, preferred_element_type=F32).astype(BF)
        y_ref[:, :width] = main
        y_ref[:, width:] = total


def combine_kernel(experts, cap, s_ref, choice_ref, gate_ref, *refs):
    returned, o_ref = refs[:-1], refs[-1]
    t, width = s_ref.shape
    choices = choice_ref[...]
    expert_at = lax.broadcasted_iota(jnp.int32, (t, 128), 1)
    first, second = expert_at == choices[:, 0:1], expert_at == choices[:, 1:2]
    earlier = lax.broadcasted_iota(jnp.int32, (t, t), 1) < lax.broadcasted_iota(
        jnp.int32, (t, t), 0
    )
    before = jnp.dot(
        earlier.astype(F32).astype(BF),
        (first | second).astype(F32).astype(BF),
        preferred_element_type=F32,
    ).astype(jnp.int32)
    keys = jnp.concatenate(
        [
            choices[:, k : k + 1] * 32
            + jnp.sum(jnp.where(named, before, 0), axis=1, keepdims=True)
            for k, named in enumerate((first, second))
        ],
        axis=0,
    )
    part = cap // len(returned)
    main, extra = part * 4 // 5, part // 5
    rows = experts * main
    at = lax.broadcasted_iota(jnp.int32, (1, rows), 1)
    quarter = width // 4
    picked = jnp.zeros((2 * t, width), F32)
    for c, back in enumerate(returned):
        main_key = at // main * 32 + c * part + at % main
        pick = (main_key == keys).astype(F32).astype(BF)
        picked += jnp.dot(pick, back[:, :width], preferred_element_type=F32)
        extra_key = at // main * 32 + c * part + main + at % main // 4
        parts = []
        for q in range(4):
            pick = ((extra_key == keys) & (at % 4 == q)).astype(F32).astype(BF)
            parts.append(jnp.dot(pick, back[:, width:], preferred_element_type=F32))
        picked += jnp.concatenate(parts, axis=1)
    gates = gate_ref[...]
    mixture = gates[:, 0:1] * picked[:t] + gates[:, 1:2] * picked[t:]
    o_ref[0] = (s_ref[...] + mixture).astype(BF)


def local(kernel, out_shape, scratch=(), **more):
    return pl.pallas_call(
        kernel,
        out_shape=out_shape,
        scratch_shapes=scratch,
        compiler_params=pltpu.CompilerParams(vmem_limit_bytes=LIMIT),
        **more,
    )


def run_experts(pieces, weight_in, weight_out):
    rows, wide = pieces[0].shape
    hidden, width = weight_in.shape
    work = len(pieces) * rows * 5 // 4
    return local(
        functools.partial(expert_kernel, len(pieces)),
        [jax.ShapeDtypeStruct((rows, wide), BF)] * len(pieces),
        [pltpu.VMEM((work, width), BF)],
        cost_estimate=pl.CostEstimate(
            flops=4 * work * hidden * width,
            bytes_accessed=4 * hidden * width + 4 * len(pieces) * rows * wide,
            transcendentals=work * hidden,
        ),
    )(weight_in, weight_out, *pieces)


def add(*parts):
    return sum(p.astype(F32) for p in parts).astype(BF)


def hop(x, axis):
    n, experts = lax.axis_size(axis), lax.axis_size("expert")
    perm = [
        (i * experts + e, (i + 1 - 2 * (e % 2)) % n * experts + e)
        for i in range(n)
        for e in range(experts)
    ]
    return lax.ppermute(x, (axis, "expert"), perm)


def after(x, *others):
    return lax.optimization_barrier((x, *others))[0]


def gather_rows(x):
    half = x.shape[0] // 2
    rows = [[x[:half], x[half:]]]
    for _ in range(lax.axis_size("dp") - 1):
        rows.append([hop(part, "dp") for part in rows[-1]])
    return rows


def expert_layer(rows, weights):
    own, *others = rows
    totals = None
    for parts in others:
        partials = run_experts(parts, *weights)
        if totals is not None:
            partials = [add(p, total) for p, total in zip(partials, totals)]
        totals = [hop(p, "dp") for p in partials]
    partials = run_experts(own, *weights)
    return jnp.concatenate([add(p, total) for p, total in zip(partials, totals)])


def per_device(
    projected,
    residual_in,
    modulation_scale,
    modulation_shift,
    expert_choice,
    gate_values,
    expert_in,
    expert_out,
):
    _, _, t, width = projected.shape
    n = lax.axis_size("ctx")
    experts = lax.axis_size("expert")
    cap = 5 * t * 2 // (4 * experts)
    slice_rows = expert_in.shape[1]
    packed = local(pack_kernel, jax.ShapeDtypeStruct((n, t * 9 // 2, 128), BF))(projected)
    block = local(join_kernel, jax.ShapeDtypeStruct((2 * slice_rows, width), BF))(
        expert_in, expert_out
    )
    mixed = lax.all_to_all(packed, "ctx", 0, 0, tiled=True)
    group = 2
    head_output = local(
        attend_kernel,
        jax.ShapeDtypeStruct((n, t * 3 // 2, 128), BF),
        [pltpu.VMEM((n * t, 128), BF)],
        grid=(n // group,),
        in_specs=[pl.BlockSpec((n, t * 9 // 2, 128), lambda i: (0, 0, 0))],
        out_specs=pl.BlockSpec((group, t * 3 // 2, 128), lambda i: (i, 0, 0)),
    )(mixed)
    back = lax.all_to_all(head_output, "ctx", 0, 0, tiled=True)
    part = cap // CHUNKS
    wide = (experts * part * 4 // 5, width * 5 // 4)
    stream, *sends = local(
        functools.partial(dispatch_kernel, experts, cap),
        [jax.ShapeDtypeStruct((t, width), F32)] + [jax.ShapeDtypeStruct(wide, BF)] * CHUNKS,
    )(back, residual_in[0], modulation_scale, modulation_shift, expert_choice[0].T)
    arrived = [lax.all_to_all(x, "expert", 0, 0, tiled=True) for x in sends]
    rows = gather_rows(arrived[0])
    gates = {0: [mixed], 1: sends, n - 2: rows[1]}
    blocks = [block]
    for step in range(n - 1):
        last = after(blocks[-1], *gates.get(step, ()))
        blocks.append(hop(last, "ctx"))
    weights = local(
        assemble_kernel, [jax.ShapeDtypeStruct((n * slice_rows, width), BF)] * 2
    )(*blocks)
    sums = [expert_layer(rows, weights)]
    returned = [lax.all_to_all(x, "expert", 0, 0, tiled=True) for x in sums]
    return local(
        functools.partial(combine_kernel, experts, cap),
        jax.ShapeDtypeStruct((1, t, width), BF),
    )(stream, expert_choice[0], gate_values[0], *returned)


def solution(mesh):
    return jax.shard_map(
        per_device,
        mesh=mesh,
        in_specs=(
            P(("dp", "expert"), None, "ctx", None),
            P(("dp", "expert"), "ctx", None),
            P(("dp", "expert"), None),
            P(("dp", "expert"), None),
            P(("dp", "expert"), "ctx", None),
            P(("dp", "expert"), "ctx", None),
            P("expert", ("dp", "ctx"), None),
            P("expert", ("dp", "ctx"), None),
        ),
        out_specs=P(("dp", "expert"), "ctx", None),
        check_vma=False,
    )
```

```python
import functools

import jax
import jax.numpy as jnp
from jax import lax
from jax.experimental import pallas as pl
from jax.experimental.pallas import tpu as pltpu
from jax.sharding import PartitionSpec as P

HD = 64
CHUNKS = 1
BF = jnp.bfloat16
F32 = jnp.float32
LIMIT = 24 * 1024 * 1024


def swap(x):
    return jnp.concatenate([x[:, HD:], x[:, :HD]], axis=1)


def low_lanes(rows):
    return lax.broadcasted_iota(jnp.int32, (rows, 2 * HD), 1) < HD


def join_kernel(in_ref, out_ref, w_ref):
    w_ref[: in_ref.shape[1], :] = in_ref[0]
    w_ref[in_ref.shape[1] :, :] = out_ref[0]


def pack_kernel(x_ref, o_ref):
    n = o_ref.shape[0]
    t = x_ref.shape[2]
    half = t // 2
    low, low_half = low_lanes(t), low_lanes(half)
    for j in range(n):
        for part in range(3):
            o_ref[j, part * t : (part + 1) * t, :] = x_ref[0, part, :, 128 * j : 128 * (j + 1)]
        at = 128 * (n + j // 2)
        q, k, v = (x_ref[0, part, :, at : at + 128] for part in range(3))
        if j % 2 == 0:
            o_ref[j, 3 * t : 4 * t, :] = jnp.where(low, q, swap(k))
            o_ref[j, 4 * t :, :] = jnp.where(low_half, v[:half], swap(v[half:]))
        else:
            o_ref[j, 3 * t : 4 * t, :] = jnp.where(low, swap(q), k)
            o_ref[j, 4 * t :, :] = jnp.where(low_half, swap(v[:half]), v[half:])


def attend_kernel(m_ref, o_ref, v2_ref):
    n, _, _ = m_ref.shape
    t = m_ref.shape[1] * 2 // 9
    half = t // 2
    group = o_ref.shape[0]
    step = pl.program_id(0)

    @pl.when(step == 0)
    def _():
        for z in range(n):
            block = m_ref[z, 4 * t :, :]
            v2_ref[z * t : z * t + half, :] = block
            v2_ref[z * t + half : (z + 1) * t, :] = swap(block)

    rows = group * t
    low = low_lanes(rows)
    mine = pl.ds(step * group, group)
    scaling = jnp.asarray(HD ** (-0.5), BF)
    q01 = m_ref[mine, 0:t, :].reshape(rows, 128) * scaling
    q2 = swap(m_ref[mine, 3 * t : 4 * t, :].reshape(rows, 128)) * scaling
    k01 = m_ref[:, t : 2 * t, :].reshape(n * t, 128)
    k2 = m_ref[:, 3 * t : 4 * t, :].reshape(n * t, 128)
    v01 = m_ref[:, 2 * t : 3 * t, :].reshape(n * t, 128)
    v2 = v2_ref[...]
    zero = jnp.zeros_like(q01)

    def head(q, k, v):
        scores = lax.dot_general(q, k, (((1,), (1,)), ((), ())), preferred_element_type=F32)
        probs = jnp.exp(scores - jnp.max(scores, axis=-1, keepdims=True))
        totals = jnp.sum(probs, axis=-1, keepdims=True)
        return jnp.dot(probs.astype(BF), v, preferred_element_type=F32) / totals

    a = head(jnp.where(low, q01, zero), k01, v01)
    b = head(jnp.where(low, zero, q01), k01, v01)
    c = head(jnp.where(low, zero, q2), k2, v2).astype(BF)
    pair = jnp.where(low, a, b).astype(BF)
    low_half = low_lanes(half)
    for g in range(group):
        o_ref[g, 0:t, :] = pair[g * t : (g + 1) * t]
        o_ref[g, t:, :] = jnp.where(
            low_half, c[g * t : g * t + half], swap(c[g * t + half : (g + 1) * t])
        )


def dispatch_kernel(experts, cap, b_ref, r_ref, scale_ref, shift_ref, choice_ref, s_ref, *sends):
    n = b_ref.shape[0]
    t, width = r_ref.shape
    half = t // 2
    low_half = low_lanes(half)
    tiles = [b_ref[j, 0:t, :] for j in range(n)]
    for m in range(n // 2):
        even, odd = b_ref[2 * m, t:, :], b_ref[2 * m + 1, t:, :]
        top = jnp.where(low_half, even, swap(odd))
        bottom = jnp.where(low_half, swap(even), odd)
        tiles.append(jnp.concatenate([top, bottom], axis=0))
    attended = jnp.concatenate(tiles, axis=1)
    stream = r_ref[...].astype(F32) + attended.astype(F32)
    s_ref[...] = stream
    mean_square = jnp.mean(stream * stream, axis=-1, keepdims=True)
    normed = (
        stream / jnp.sqrt(mean_square + 1e-06) * (1.0 + scale_ref[...]) + shift_ref[...]
    ).astype(BF)
    choices = choice_ref[...]
    expert_at = lax.broadcasted_iota(jnp.int32, (experts, t), 0)
    first, second = expert_at == choices[0:1], expert_at == choices[1:2]
    earlier = lax.broadcasted_iota(jnp.int32, (t, t), 0) < lax.broadcasted_iota(
        jnp.int32, (t, t), 1
    )
    before = jnp.dot(
        (first | second).astype(F32).astype(BF),
        earlier.astype(F32).astype(BF),
        preferred_element_type=F32,
    ).astype(jnp.int32)
    keys = [
        choices[k : k + 1] * 32 + jnp.sum(jnp.where(named, before, 0), axis=0, keepdims=True)
        for k, named in enumerate((first, second))
    ]
    part = cap // len(sends)
    main, extra = part * 4 // 5, part // 5
    rows = experts * main
    at = lax.broadcasted_iota(jnp.int32, (rows, 1), 0)
    quarter = width // 4
    for c, send in enumerate(sends):
        main_key = at // main * 32 + c * part + at % main
        pick = ((main_key == keys[0]) | (main_key == keys[1])).astype(F32).astype(BF)
        send[:, :width] = jnp.dot(pick, normed, preferred_element_type=F32).astype(BF)
        extra_key = at // main * 32 + c * part + main + at % main // 4
        matches = (extra_key == keys[0]) | (extra_key == keys[1])
        total = jnp.zeros((rows, quarter), F32)
        for q in range(4):
            pick = (matches & (at % 4 == q)).astype(F32).astype(BF)
            total += jnp.dot(
                pick, normed[:, q * quarter : (q + 1) * quarter], preferred_element_type=F32
            )
        send[:, width:] = total.astype(BF)


def assemble_kernel(*refs):
    far_in, far_out, *blocks, in_ref, out_ref = refs
    rows = far_in.shape[0]
    in_ref[len(blocks) * rows :, :] = far_in[...]
    out_ref[len(blocks) * rows :, :] = far_out[...]
    for i, block in enumerate(blocks):
        in_ref[i * rows : (i + 1) * rows, :] = block[:rows, :]
        out_ref[i * rows : (i + 1) * rows, :] = block[rows:, :]


def expert_kernel(pieces, in_ref, out_ref, *refs):
    x_refs, plus, y_refs, rows_ref = refs[:pieces], refs[pieces : -pieces - 1], refs[-pieces - 1 : -1], refs[-1]
    rows = x_refs[0].shape[0]
    width = in_ref.shape[1]
    quarter = width // 4
    extras = rows // 4
    every = rows + extras
    row_at = lax.broadcasted_iota(jnp.int32, (rows, rows), 0)
    source = lax.broadcasted_iota(jnp.int32, (rows, rows), 1)
    pick = (source == 4 * (row_at % extras) + row_at // extras).astype(F32).astype(BF)
    for p, x_ref in enumerate(x_refs):
        base = p * every
        rows_ref[base : base + rows, :] = x_ref[:, :width]
        quarters = jnp.dot(pick, x_ref[:, width:], preferred_element_type=F32).astype(BF)
        for q in range(4):
            rows_ref[base + rows : base + every, q * quarter : (q + 1) * quarter] = quarters[
                q * extras : (q + 1) * extras
            ]
    pre_act = lax.dot_general(
        rows_ref[...], in_ref[...], (((1,), (1,)), ((), ())), preferred_element_type=F32
    )
    hidden = jax.nn.gelu(pre_act, approximate=True).astype(BF)
    partial = jnp.dot(hidden, out_ref[...], preferred_element_type=F32).astype(BF)
    pack = (row_at == 4 * (source % extras) + source // extras).astype(F32).astype(BF)
    for p, y_ref in enumerate(y_refs):
        base = p * every
        main = partial[base : base + rows]
        last = partial[base + rows : base + every]
        quarters = jnp.concatenate(
            [last[:, q * quarter : (q + 1) * quarter] for q in range(4)], axis=0
        )
        total = jnp.dot(pack, quarters, preferred_element_type=F32).astype(BF)
        if plus:
            main = add(main, plus[p][:, :width])
            total = add(total, plus[p][:, width:])
        y_ref[:, :width] = main
        y_ref[:, width:] = total


def combine_kernel(experts, cap, s_ref, choice_ref, gate_ref, *refs):
    returned, o_ref = refs[:-1], refs[-1]
    t, width = s_ref.shape
    choices = choice_ref[...]
    expert_at = lax.broadcasted_iota(jnp.int32, (t, 128), 1)
    first, second = expert_at == choices[:, 0:1], expert_at == choices[:, 1:2]
    earlier = lax.broadcasted_iota(jnp.int32, (t, t), 1) < lax.broadcasted_iota(
        jnp.int32, (t, t), 0
    )
    before = jnp.dot(
        earlier.astype(F32).astype(BF),
        (first | second).astype(F32).astype(BF),
        preferred_element_type=F32,
    ).astype(jnp.int32)
    keys = jnp.concatenate(
        [
            choices[:, k : k + 1] * 32
            + jnp.sum(jnp.where(named, before, 0), axis=1, keepdims=True)
            for k, named in enumerate((first, second))
        ],
        axis=0,
    )
    part = cap // len(returned)
    main, extra = part * 4 // 5, part // 5
    rows = experts * main
    at = lax.broadcasted_iota(jnp.int32, (1, rows), 1)
    quarter = width // 4
    picked = jnp.zeros((2 * t, width), F32)
    for c, back in enumerate(returned):
        main_key = at // main * 32 + c * part + at % main
        pick = (main_key == keys).astype(F32).astype(BF)
        picked += jnp.dot(pick, back[:, :width], preferred_element_type=F32)
        extra_key = at // main * 32 + c * part + main + at % main // 4
        parts = []
        for q in range(4):
            pick = ((extra_key == keys) & (at % 4 == q)).astype(F32).astype(BF)
            parts.append(jnp.dot(pick, back[:, width:], preferred_element_type=F32))
        picked += jnp.concatenate(parts, axis=1)
    gates = gate_ref[...]
    mixture = gates[:, 0:1] * picked[:t] + gates[:, 1:2] * picked[t:]
    o_ref[0] = (s_ref[...] + mixture).astype(BF)


def local(kernel, out_shape, scratch=(), **more):
    return pl.pallas_call(
        kernel,
        out_shape=out_shape,
        scratch_shapes=scratch,
        compiler_params=pltpu.CompilerParams(vmem_limit_bytes=LIMIT),
        **more,
    )


def run_experts(pieces, weight_in, weight_out, plus=()):
    rows, wide = pieces[0].shape
    hidden, width = weight_in.shape
    work = len(pieces) * rows * 5 // 4
    return local(
        functools.partial(expert_kernel, len(pieces)),
        [jax.ShapeDtypeStruct((rows, wide), BF)] * len(pieces),
        [pltpu.VMEM((work, width), BF)],
        cost_estimate=pl.CostEstimate(
            flops=4 * work * hidden * width,
            bytes_accessed=4 * hidden * width + 4 * len(pieces) * rows * wide,
            transcendentals=work * hidden,
        ),
    )(weight_in, weight_out, *pieces, *plus)


def add(*parts):
    return sum(p.astype(F32) for p in parts).astype(BF)


def shift(x, axis, by):
    n = lax.axis_size(axis)
    return lax.ppermute(x, axis, [(i, (i + by) % n) for i in range(n)])


def after(x, *others):
    return lax.optimization_barrier((x, *others))[0]


def ring_in(x):
    half = x.shape[0] // 2
    a, b = x[:half], x[half:]
    left_a, right_b = shift(a, "dp", 1), shift(b, "dp", -1)
    left_b, right_a = shift(b, "dp", 1), shift(a, "dp", -1)
    across_a, across_b = shift(left_a, "dp", 1), shift(right_b, "dp", -1)
    return (a, b), (left_a, left_b, right_a, right_b), (across_a, across_b)


def expert_layer(own, near, across, weights):
    to_left_a, to_left_b, to_right_a, to_right_b = run_experts(near, *weights)
    got_a, got_b = shift(to_left_a, "dp", -1), shift(to_right_b, "dp", 1)
    across = after(across, to_left_a)
    to_across_a, to_across_b = run_experts(across, *weights)
    via_a, via_b = shift(to_across_a, "dp", 1), shift(to_across_b, "dp", -1)
    via_a, via_b = add(to_right_a, via_a), add(to_left_b, via_b)
    sum_a, sum_b = shift(via_a, "dp", 1), shift(via_b, "dp", -1)
    own = after(own, via_a, via_b)
    own_a, own_b = run_experts(own, *weights, plus=(got_a, got_b))
    return jnp.concatenate([add(own_a, sum_a), add(own_b, sum_b)])


def per_device(
    projected,
    residual_in,
    modulation_scale,
    modulation_shift,
    expert_choice,
    gate_values,
    expert_in,
    expert_out,
):
    _, _, t, width = projected.shape
    n = lax.axis_size("ctx")
    experts = lax.axis_size("expert")
    cap = 5 * t * 2 // (4 * experts)
    slice_rows = expert_in.shape[1]
    packed = local(pack_kernel, jax.ShapeDtypeStruct((n, t * 9 // 2, 128), BF))(projected)
    block = local(join_kernel, jax.ShapeDtypeStruct((2 * slice_rows, width), BF))(
        expert_in, expert_out
    )
    mixed = lax.all_to_all(packed, "ctx", 0, 0, tiled=True)
    up, down = [shift(block, "ctx", 1)], [shift(block, "ctx", -1)]
    mixed, up[0], down[0] = lax.optimization_barrier((mixed, up[0], down[0]))
    group = 2
    head_output = local(
        attend_kernel,
        jax.ShapeDtypeStruct((n, t * 3 // 2, 128), BF),
        [pltpu.VMEM((n * t, 128), BF)],
        grid=(n // group,),
        in_specs=[pl.BlockSpec((n, t * 9 // 2, 128), lambda i: (0, 0, 0))],
        out_specs=pl.BlockSpec((group, t * 3 // 2, 128), lambda i: (i, 0, 0)),
    )(mixed)
    back = lax.all_to_all(head_output, "ctx", 0, 0, tiled=True)
    part = cap // CHUNKS
    wide = (experts * part * 4 // 5, width * 5 // 4)
    stream, *sends = local(
        functools.partial(dispatch_kernel, experts, cap),
        [jax.ShapeDtypeStruct((t, width), F32)] + [jax.ShapeDtypeStruct(wide, BF)] * CHUNKS,
    )(back, residual_in[0], modulation_scale, modulation_shift, expert_choice[0].T)
    up[0], down[0] = after(up[0], *sends), after(down[0], *sends)
    arrived = [lax.all_to_all(x, "expert", 0, 0, tiled=True) for x in sends]
    for _ in range(n // 2 - 2):
        up.append(shift(up[-1], "ctx", 1))
        down.append(shift(down[-1], "ctx", -1))
    ring = ring_in(*arrived)
    up[-1], down[-1] = after((up[-1], down[-1]), ring[0])
    far_in = shift(up[-1][:slice_rows], "ctx", 1)
    far_out = shift(down[-1][slice_rows:], "ctx", -1)
    weights = local(
        assemble_kernel, [jax.ShapeDtypeStruct((n * slice_rows, width), BF)] * 2
    )(far_in, far_out, block, *up, *down)
    sums = [expert_layer(*ring, weights)]
    returned = [lax.all_to_all(x, "expert", 0, 0, tiled=True) for x in sums]
    return local(
        functools.partial(combine_kernel, experts, cap),
        jax.ShapeDtypeStruct((1, t, width), BF),
    )(stream, expert_choice[0], gate_values[0], *returned)


def solution(mesh):
    return jax.shard_map(
        per_device,
        mesh=mesh,
        in_specs=(
            P(("dp", "expert"), None, "ctx", None),
            P(("dp", "expert"), "ctx", None),
            P(("dp", "expert"), None),
            P(("dp", "expert"), None),
            P(("dp", "expert"), "ctx", None),
            P(("dp", "expert"), "ctx", None),
            P("expert", ("dp", "ctx"), None),
            P("expert", ("dp", "ctx"), None),
        ),
        out_specs=P(("dp", "expert"), "ctx", None),
        check_vma=False,
    )
```

```python
import functools

import jax
import jax.numpy as jnp
from jax import lax
from jax.experimental import pallas as pl
from jax.experimental.pallas import tpu as pltpu
from jax.sharding import PartitionSpec as P

HD = 64
CHUNKS = 1
BF = jnp.bfloat16
F32 = jnp.float32
LIMIT = 24 * 1024 * 1024


def swap(x):
    return jnp.concatenate([x[:, HD:], x[:, :HD]], axis=1)


def low_lanes(rows):
    return lax.broadcasted_iota(jnp.int32, (rows, 2 * HD), 1) < HD


def join_kernel(in_ref, out_ref, w_ref):
    w_ref[: in_ref.shape[1], :] = in_ref[0]
    w_ref[in_ref.shape[1] :, :] = out_ref[0]


def pack_kernel(x_ref, o_ref):
    n = o_ref.shape[0]
    t = x_ref.shape[2]
    half = t // 2
    low, low_half = low_lanes(t), low_lanes(half)
    for j in range(n):
        for part in range(3):
            o_ref[j, part * t : (part + 1) * t, :] = x_ref[0, part, :, 128 * j : 128 * (j + 1)]
        at = 128 * (n + j // 2)
        q, k, v = (x_ref[0, part, :, at : at + 128] for part in range(3))
        if j % 2 == 0:
            o_ref[j, 3 * t : 4 * t, :] = jnp.where(low, q, swap(k))
            o_ref[j, 4 * t :, :] = jnp.where(low_half, v[:half], swap(v[half:]))
        else:
            o_ref[j, 3 * t : 4 * t, :] = jnp.where(low, swap(q), k)
            o_ref[j, 4 * t :, :] = jnp.where(low_half, swap(v[:half]), v[half:])


def attend_kernel(m_ref, o_ref, v2_ref):
    n, _, _ = m_ref.shape
    t = m_ref.shape[1] * 2 // 9
    half = t // 2
    group = o_ref.shape[0]
    step = pl.program_id(0)

    @pl.when(step == 0)
    def _():
        for z in range(n):
            block = m_ref[z, 4 * t :, :]
            v2_ref[z * t : z * t + half, :] = block
            v2_ref[z * t + half : (z + 1) * t, :] = swap(block)

    rows = group * t
    low = low_lanes(rows)
    mine = pl.ds(step * group, group)
    scaling = jnp.asarray(HD ** (-0.5), BF)
    q01 = m_ref[mine, 0:t, :].reshape(rows, 128) * scaling
    q2 = swap(m_ref[mine, 3 * t : 4 * t, :].reshape(rows, 128)) * scaling
    k01 = m_ref[:, t : 2 * t, :].reshape(n * t, 128)
    k2 = m_ref[:, 3 * t : 4 * t, :].reshape(n * t, 128)
    v01 = m_ref[:, 2 * t : 3 * t, :].reshape(n * t, 128)
    v2 = v2_ref[...]
    zero = jnp.zeros_like(q01)

    def head(q, k, v):
        scores = lax.dot_general(q, k, (((1,), (1,)), ((), ())), preferred_element_type=F32)
        probs = jnp.exp(scores - jnp.max(scores, axis=-1, keepdims=True))
        totals = jnp.sum(probs, axis=-1, keepdims=True)
        return jnp.dot(probs.astype(BF), v, preferred_element_type=F32) / totals

    a = head(jnp.where(low, q01, zero), k01, v01)
    b = head(jnp.where(low, zero, q01), k01, v01)
    c = head(jnp.where(low, zero, q2), k2, v2).astype(BF)
    pair = jnp.where(low, a, b).astype(BF)
    low_half = low_lanes(half)
    for g in range(group):
        o_ref[g, 0:t, :] = pair[g * t : (g + 1) * t]
        o_ref[g, t:, :] = jnp.where(
            low_half, c[g * t : g * t + half], swap(c[g * t + half : (g + 1) * t])
        )


def dispatch_kernel(experts, cap, b_ref, r_ref, scale_ref, shift_ref, choice_ref, s_ref, *sends):
    n = b_ref.shape[0]
    t, width = r_ref.shape
    half = t // 2
    low_half = low_lanes(half)
    tiles = [b_ref[j, 0:t, :] for j in range(n)]
    for m in range(n // 2):
        even, odd = b_ref[2 * m, t:, :], b_ref[2 * m + 1, t:, :]
        top = jnp.where(low_half, even, swap(odd))
        bottom = jnp.where(low_half, swap(even), odd)
        tiles.append(jnp.concatenate([top, bottom], axis=0))
    attended = jnp.concatenate(tiles, axis=1)
    stream = r_ref[...].astype(F32) + attended.astype(F32)
    s_ref[...] = stream
    mean_square = jnp.mean(stream * stream, axis=-1, keepdims=True)
    normed = (
        stream / jnp.sqrt(mean_square + 1e-06) * (1.0 + scale_ref[...]) + shift_ref[...]
    ).astype(BF)
    choices = choice_ref[...]
    expert_at = lax.broadcasted_iota(jnp.int32, (experts, t), 0)
    first, second = expert_at == choices[0:1], expert_at == choices[1:2]
    earlier = lax.broadcasted_iota(jnp.int32, (t, t), 0) < lax.broadcasted_iota(
        jnp.int32, (t, t), 1
    )
    before = jnp.dot(
        (first | second).astype(F32).astype(BF),
        earlier.astype(F32).astype(BF),
        preferred_element_type=F32,
    ).astype(jnp.int32)
    keys = [
        choices[k : k + 1] * 32 + jnp.sum(jnp.where(named, before, 0), axis=0, keepdims=True)
        for k, named in enumerate((first, second))
    ]
    part = cap // len(sends)
    main, extra = part * 4 // 5, part // 5
    rows = experts * main
    at = lax.broadcasted_iota(jnp.int32, (rows, 1), 0)
    quarter = width // 4
    for c, send in enumerate(sends):
        main_key = at // main * 32 + c * part + at % main
        pick = ((main_key == keys[0]) | (main_key == keys[1])).astype(F32).astype(BF)
        send[:, :width] = jnp.dot(pick, normed, preferred_element_type=F32).astype(BF)
        extra_key = at // main * 32 + c * part + main + at % main // 4
        matches = (extra_key == keys[0]) | (extra_key == keys[1])
        total = jnp.zeros((rows, quarter), F32)
        for q in range(4):
            pick = (matches & (at % 4 == q)).astype(F32).astype(BF)
            total += jnp.dot(
                pick, normed[:, q * quarter : (q + 1) * quarter], preferred_element_type=F32
            )
        send[:, width:] = total.astype(BF)


def assemble_kernel(*refs):
    far_in, far_out, *blocks, in_ref, out_ref = refs
    rows = far_in.shape[0]
    in_ref[len(blocks) * rows :, :] = far_in[...]
    out_ref[len(blocks) * rows :, :] = far_out[...]
    for i, block in enumerate(blocks):
        in_ref[i * rows : (i + 1) * rows, :] = block[:rows, :]
        out_ref[i * rows : (i + 1) * rows, :] = block[rows:, :]


def expert_kernel(pieces, in_ref, out_ref, *refs):
    x_refs, plus, y_refs, rows_ref = refs[:pieces], refs[pieces : -pieces - 1], refs[-pieces - 1 : -1], refs[-1]
    rows = x_refs[0].shape[0]
    width = in_ref.shape[1]
    quarter = width // 4
    extras = rows // 4
    every = rows + extras
    row_at = lax.broadcasted_iota(jnp.int32, (rows, rows), 0)
    source = lax.broadcasted_iota(jnp.int32, (rows, rows), 1)
    pick = (source == 4 * (row_at % extras) + row_at // extras).astype(F32).astype(BF)
    for p, x_ref in enumerate(x_refs):
        base = p * every
        rows_ref[base : base + rows, :] = x_ref[:, :width]
        quarters = jnp.dot(pick, x_ref[:, width:], preferred_element_type=F32).astype(BF)
        for q in range(4):
            rows_ref[base + rows : base + every, q * quarter : (q + 1) * quarter] = quarters[
                q * extras : (q + 1) * extras
            ]
    pre_act = lax.dot_general(
        rows_ref[...], in_ref[...], (((1,), (1,)), ((), ())), preferred_element_type=F32
    )
    hidden = jax.nn.gelu(pre_act, approximate=True).astype(BF)
    partial = jnp.dot(hidden, out_ref[...], preferred_element_type=F32).astype(BF)
    pack = (row_at == 4 * (source % extras) + source // extras).astype(F32).astype(BF)
    for p, y_ref in enumerate(y_refs):
        base = p * every
        main = partial[base : base + rows]
        last = partial[base + rows : base + every]
        quarters = jnp.concatenate(
            [last[:, q * quarter : (q + 1) * quarter] for q in range(4)], axis=0
        )
        total = jnp.dot(pack, quarters, preferred_element_type=F32).astype(BF)
        if plus:
            main = add(main, plus[p][:, :width])
            total = add(total, plus[p][:, width:])
        y_ref[:, :width] = main
        y_ref[:, width:] = total


def combine_kernel(experts, cap, s_ref, choice_ref, gate_ref, *refs):
    returned, o_ref = refs[:-1], refs[-1]
    t, width = s_ref.shape
    choices = choice_ref[...]
    expert_at = lax.broadcasted_iota(jnp.int32, (t, 128), 1)
    first, second = expert_at == choices[:, 0:1], expert_at == choices[:, 1:2]
    earlier = lax.broadcasted_iota(jnp.int32, (t, t), 1) < lax.broadcasted_iota(
        jnp.int32, (t, t), 0
    )
    before = jnp.dot(
        earlier.astype(F32).astype(BF),
        (first | second).astype(F32).astype(BF),
        preferred_element_type=F32,
    ).astype(jnp.int32)
    keys = jnp.concatenate(
        [
            choices[:, k : k + 1] * 32
            + jnp.sum(jnp.where(named, before, 0), axis=1, keepdims=True)
            for k, named in enumerate((first, second))
        ],
        axis=0,
    )
    part = cap // len(returned)
    main, extra = part * 4 // 5, part // 5
    rows = experts * main
    at = lax.broadcasted_iota(jnp.int32, (1, rows), 1)
    quarter = width // 4
    picked = jnp.zeros((2 * t, width), F32)
    for c, back in enumerate(returned):
        main_key = at // main * 32 + c * part + at % main
        pick = (main_key == keys).astype(F32).astype(BF)
        picked += jnp.dot(pick, back[:, :width], preferred_element_type=F32)
        extra_key = at // main * 32 + c * part + main + at % main // 4
        parts = []
        for q in range(4):
            pick = ((extra_key == keys) & (at % 4 == q)).astype(F32).astype(BF)
            parts.append(jnp.dot(pick, back[:, width:], preferred_element_type=F32))
        picked += jnp.concatenate(parts, axis=1)
    gates = gate_ref[...]
    mixture = gates[:, 0:1] * picked[:t] + gates[:, 1:2] * picked[t:]
    o_ref[0] = (s_ref[...] + mixture).astype(BF)


def local(kernel, out_shape, scratch=(), **more):
    return pl.pallas_call(
        kernel,
        out_shape=out_shape,
        scratch_shapes=scratch,
        compiler_params=pltpu.CompilerParams(vmem_limit_bytes=LIMIT),
        **more,
    )


def run_experts(pieces, weight_in, weight_out, plus=()):
    rows, wide = pieces[0].shape
    hidden, width = weight_in.shape
    work = len(pieces) * rows * 5 // 4
    return local(
        functools.partial(expert_kernel, len(pieces)),
        [jax.ShapeDtypeStruct((rows, wide), BF)] * len(pieces),
        [pltpu.VMEM((work, width), BF)],
        cost_estimate=pl.CostEstimate(
            flops=4 * work * hidden * width,
            bytes_accessed=4 * hidden * width + 4 * len(pieces) * rows * wide,
            transcendentals=work * hidden,
        ),
    )(weight_in, weight_out, *pieces, *plus)


def add(*parts):
    return sum(p.astype(F32) for p in parts).astype(BF)


def shift(x, axis, by):
    n = lax.axis_size(axis)
    return lax.ppermute(x, axis, [(i, (i + by) % n) for i in range(n)])


def after(x, *others):
    return lax.optimization_barrier((x, *others))[0]


def ring_in(x):
    half = x.shape[0] // 2
    a, b = x[:half], x[half:]
    left_a, right_b = shift(a, "dp", 1), shift(b, "dp", -1)
    left_b, right_a = shift(b, "dp", 1), shift(a, "dp", -1)
    across_a, across_b = shift(left_a, "dp", 1), shift(right_b, "dp", -1)
    return (a, b), (left_a, left_b, right_a, right_b), (across_a, across_b)


def expert_layer(own, near, across, weights):
    to_left_a, to_left_b, to_right_a, to_right_b = run_experts(near, *weights)
    got_a, got_b = shift(to_left_a, "dp", -1), shift(to_right_b, "dp", 1)
    across = after(across, to_left_a)
    to_across_a, to_across_b = run_experts(across, *weights)
    via_a, via_b = shift(to_across_a, "dp", 1), shift(to_across_b, "dp", -1)
    via_a, via_b = add(to_right_a, via_a), add(to_left_b, via_b)
    sum_a, sum_b = shift(via_a, "dp", 1), shift(via_b, "dp", -1)
    own = after(own, via_a, via_b)
    own_a, own_b = run_experts(own, *weights, plus=(got_a, got_b))
    return jnp.concatenate([add(own_a, sum_a), add(own_b, sum_b)])


def per_device(
    projected,
    residual_in,
    modulation_scale,
    modulation_shift,
    expert_choice,
    gate_values,
    expert_in,
    expert_out,
):
    _, _, t, width = projected.shape
    n = lax.axis_size("ctx")
    experts = lax.axis_size("expert")
    cap = 5 * t * 2 // (4 * experts)
    slice_rows = expert_in.shape[1]
    packed = local(pack_kernel, jax.ShapeDtypeStruct((n, t * 9 // 2, 128), BF))(projected)
    block = local(join_kernel, jax.ShapeDtypeStruct((2 * slice_rows, width), BF))(
        expert_in, expert_out
    )
    mixed = lax.all_to_all(packed, "ctx", 0, 0, tiled=True)
    group = 4
    head_output = local(
        attend_kernel,
        jax.ShapeDtypeStruct((n, t * 3 // 2, 128), BF),
        [pltpu.VMEM((n * t, 128), BF)],
        grid=(n // group,),
        in_specs=[pl.BlockSpec((n, t * 9 // 2, 128), lambda i: (0, 0, 0))],
        out_specs=pl.BlockSpec((group, t * 3 // 2, 128), lambda i: (i, 0, 0)),
    )(mixed)
    back = lax.all_to_all(head_output, "ctx", 0, 0, tiled=True)
    part = cap // CHUNKS
    wide = (experts * part * 4 // 5, width * 5 // 4)
    stream, *sends = local(
        functools.partial(dispatch_kernel, experts, cap),
        [jax.ShapeDtypeStruct((t, width), F32)] + [jax.ShapeDtypeStruct(wide, BF)] * CHUNKS,
    )(back, residual_in[0], modulation_scale, modulation_shift, expert_choice[0].T)
    first = after(block, mixed)
    up, down = [shift(first, "ctx", 1)], [shift(first, "ctx", -1)]
    *sends, up[0], down[0] = lax.optimization_barrier((*sends, up[0], down[0]))
    arrived = [lax.all_to_all(x, "expert", 0, 0, tiled=True) for x in sends]
    ring = ring_in(*arrived)
    up.append(shift(up[-1], "ctx", 1))
    down.append(shift(down[-1], "ctx", -1))
    up.append(shift(up[-1], "ctx", 1))
    down.append(shift(down[-1], "ctx", -1))
    up[-1], down[-1] = after((up[-1], down[-1]), ring[0])
    far_in = shift(up[-1][:slice_rows], "ctx", 1)
    far_out = shift(down[-1][slice_rows:], "ctx", -1)
    weights = local(
        assemble_kernel,
        [jax.ShapeDtypeStruct((n * slice_rows, width), BF)] * 2,

    )(far_in, far_out, block, *up, *down)
    sums = [expert_layer(*ring, weights)]
    returned = [lax.all_to_all(x, "expert", 0, 0, tiled=True) for x in sums]
    return local(
        functools.partial(combine_kernel, experts, cap),
        jax.ShapeDtypeStruct((1, t, width), BF),
    )(stream, expert_choice[0], gate_values[0], *returned)


def solution(mesh):
    return jax.shard_map(
        per_device,
        mesh=mesh,
        in_specs=(
            P(("dp", "expert"), None, "ctx", None),
            P(("dp", "expert"), "ctx", None),
            P(("dp", "expert"), None),
            P(("dp", "expert"), None),
            P(("dp", "expert"), "ctx", None),
            P(("dp", "expert"), "ctx", None),
            P("expert", ("dp", "ctx"), None),
            P("expert", ("dp", "ctx"), None),
        ),
        out_specs=P(("dp", "expert"), "ctx", None),
        check_vma=False,
    )
```

```python
import functools

import jax
import jax.numpy as jnp
from jax import lax
from jax.experimental import pallas as pl
from jax.experimental.pallas import tpu as pltpu
from jax.sharding import PartitionSpec as P

HD = 64
CHUNKS = 1
BF = jnp.bfloat16
F32 = jnp.float32
LIMIT = 24 * 1024 * 1024


def swap(x):
    return jnp.concatenate([x[:, HD:], x[:, :HD]], axis=1)


def low_lanes(rows):
    return lax.broadcasted_iota(jnp.int32, (rows, 2 * HD), 1) < HD


def join_kernel(in_ref, out_ref, w_ref):
    w_ref[: in_ref.shape[1], :] = in_ref[0]
    w_ref[in_ref.shape[1] :, :] = out_ref[0]


def pack_kernel(x_ref, o_ref):
    n = o_ref.shape[0]
    t = x_ref.shape[2]
    half = t // 2
    low, low_half = low_lanes(t), low_lanes(half)
    for j in range(n):
        for part in range(3):
            o_ref[j, part * t : (part + 1) * t, :] = x_ref[0, part, :, 128 * j : 128 * (j + 1)]
        at = 128 * (n + j // 2)
        q, k, v = (x_ref[0, part, :, at : at + 128] for part in range(3))
        if j % 2 == 0:
            o_ref[j, 3 * t : 4 * t, :] = jnp.where(low, q, swap(k))
            o_ref[j, 4 * t :, :] = jnp.where(low_half, v[:half], swap(v[half:]))
        else:
            o_ref[j, 3 * t : 4 * t, :] = jnp.where(low, swap(q), k)
            o_ref[j, 4 * t :, :] = jnp.where(low_half, swap(v[:half]), v[half:])


def attend_kernel(m_ref, o_ref, v2_ref):
    n, _, _ = m_ref.shape
    t = m_ref.shape[1] * 2 // 9
    half = t // 2
    group = o_ref.shape[0]
    step = pl.program_id(0)

    @pl.when(step == 0)
    def _():
        for z in range(n):
            block = m_ref[z, 4 * t :, :]
            v2_ref[z * t : z * t + half, :] = block
            v2_ref[z * t + half : (z + 1) * t, :] = swap(block)

    rows = group * t
    low = low_lanes(rows)
    mine = pl.ds(step * group, group)
    scaling = jnp.asarray(HD ** (-0.5), BF)
    q01 = m_ref[mine, 0:t, :].reshape(rows, 128) * scaling
    q2 = swap(m_ref[mine, 3 * t : 4 * t, :].reshape(rows, 128)) * scaling
    k01 = m_ref[:, t : 2 * t, :].reshape(n * t, 128)
    k2 = m_ref[:, 3 * t : 4 * t, :].reshape(n * t, 128)
    v01 = m_ref[:, 2 * t : 3 * t, :].reshape(n * t, 128)
    v2 = v2_ref[...]
    zero = jnp.zeros_like(q01)

    def head(q, k, v):
        scores = lax.dot_general(q, k, (((1,), (1,)), ((), ())), preferred_element_type=F32)
        probs = jnp.exp(scores - jnp.max(scores, axis=-1, keepdims=True))
        totals = jnp.sum(probs, axis=-1, keepdims=True)
        return jnp.dot(probs.astype(BF), v, preferred_element_type=F32) / totals

    a = head(jnp.where(low, q01, zero), k01, v01)
    b = head(jnp.where(low, zero, q01), k01, v01)
    c = head(jnp.where(low, zero, q2), k2, v2).astype(BF)
    pair = jnp.where(low, a, b).astype(BF)
    low_half = low_lanes(half)
    for g in range(group):
        o_ref[g, 0:t, :] = pair[g * t : (g + 1) * t]
        o_ref[g, t:, :] = jnp.where(
            low_half, c[g * t : g * t + half], swap(c[g * t + half : (g + 1) * t])
        )


def dispatch_kernel(experts, cap, b_ref, r_ref, scale_ref, shift_ref, choice_ref, s_ref, *sends):
    n = b_ref.shape[0]
    t, width = r_ref.shape
    half = t // 2
    low_half = low_lanes(half)
    tiles = [b_ref[j, 0:t, :] for j in range(n)]
    for m in range(n // 2):
        even, odd = b_ref[2 * m, t:, :], b_ref[2 * m + 1, t:, :]
        top = jnp.where(low_half, even, swap(odd))
        bottom = jnp.where(low_half, swap(even), odd)
        tiles.append(jnp.concatenate([top, bottom], axis=0))
    attended = jnp.concatenate(tiles, axis=1)
    stream = r_ref[...].astype(F32) + attended.astype(F32)
    s_ref[...] = stream
    mean_square = jnp.mean(stream * stream, axis=-1, keepdims=True)
    normed = (
        stream / jnp.sqrt(mean_square + 1e-06) * (1.0 + scale_ref[...]) + shift_ref[...]
    ).astype(BF)
    choices = choice_ref[...]
    expert_at = lax.broadcasted_iota(jnp.int32, (experts, t), 0)
    first, second = expert_at == choices[0:1], expert_at == choices[1:2]
    earlier = lax.broadcasted_iota(jnp.int32, (t, t), 0) < lax.broadcasted_iota(
        jnp.int32, (t, t), 1
    )
    before = jnp.dot(
        (first | second).astype(F32).astype(BF),
        earlier.astype(F32).astype(BF),
        preferred_element_type=F32,
    ).astype(jnp.int32)
    keys = [
        choices[k : k + 1] * 32 + jnp.sum(jnp.where(named, before, 0), axis=0, keepdims=True)
        for k, named in enumerate((first, second))
    ]
    part = cap // len(sends)
    main, extra = part * 4 // 5, part // 5
    rows = experts * main
    at = lax.broadcasted_iota(jnp.int32, (rows, 1), 0)
    quarter = width // 4
    for c, send in enumerate(sends):
        main_key = at // main * 32 + c * part + at % main
        pick = ((main_key == keys[0]) | (main_key == keys[1])).astype(F32).astype(BF)
        send[:, :width] = jnp.dot(pick, normed, preferred_element_type=F32).astype(BF)
        extra_key = at // main * 32 + c * part + main + at % main // 4
        matches = (extra_key == keys[0]) | (extra_key == keys[1])
        total = jnp.zeros((rows, quarter), F32)
        for q in range(4):
            pick = (matches & (at % 4 == q)).astype(F32).astype(BF)
            total += jnp.dot(
                pick, normed[:, q * quarter : (q + 1) * quarter], preferred_element_type=F32
            )
        send[:, width:] = total.astype(BF)


def assemble_kernel(*refs):
    far_in, far_out, *blocks, in_ref, out_ref = refs
    rows = far_in.shape[0]
    in_ref[len(blocks) * rows :, :] = far_in[...]
    out_ref[len(blocks) * rows :, :] = far_out[...]
    for i, block in enumerate(blocks):
        in_ref[i * rows : (i + 1) * rows, :] = block[:rows, :]
        out_ref[i * rows : (i + 1) * rows, :] = block[rows:, :]


def relay_kernel(up_ref, down_ref, up_out_ref, down_out_ref):
    up_out_ref[...] = up_ref[...]
    down_out_ref[...] = down_ref[...]


def expert_kernel(pieces, in_ref, out_ref, *refs):
    x_refs, plus, y_refs, rows_ref = refs[:pieces], refs[pieces : -pieces - 1], refs[-pieces - 1 : -1], refs[-1]
    rows = x_refs[0].shape[0]
    width = in_ref.shape[1]
    quarter = width // 4
    extras = rows // 4
    every = rows + extras
    row_at = lax.broadcasted_iota(jnp.int32, (rows, rows), 0)
    source = lax.broadcasted_iota(jnp.int32, (rows, rows), 1)
    pick = (source == 4 * (row_at % extras) + row_at // extras).astype(F32).astype(BF)
    for p, x_ref in enumerate(x_refs):
        base = p * every
        rows_ref[base : base + rows, :] = x_ref[:, :width]
        quarters = jnp.dot(pick, x_ref[:, width:], preferred_element_type=F32).astype(BF)
        for q in range(4):
            rows_ref[base + rows : base + every, q * quarter : (q + 1) * quarter] = quarters[
                q * extras : (q + 1) * extras
            ]
    pre_act = lax.dot_general(
        rows_ref[...], in_ref[...], (((1,), (1,)), ((), ())), preferred_element_type=F32
    )
    hidden = jax.nn.gelu(pre_act, approximate=True).astype(BF)
    partial = jnp.dot(hidden, out_ref[...], preferred_element_type=F32).astype(BF)
    pack = (row_at == 4 * (source % extras) + source // extras).astype(F32).astype(BF)
    for p, y_ref in enumerate(y_refs):
        base = p * every
        main = partial[base : base + rows]
        last = partial[base + rows : base + every]
        quarters = jnp.concatenate(
            [last[:, q * quarter : (q + 1) * quarter] for q in range(4)], axis=0
        )
        total = jnp.dot(pack, quarters, preferred_element_type=F32).astype(BF)
        if plus:
            main = add(main, plus[p][:, :width])
            total = add(total, plus[p][:, width:])
        y_ref[:, :width] = main
        y_ref[:, width:] = total


def combine_kernel(experts, cap, s_ref, choice_ref, gate_ref, *refs):
    returned, o_ref = refs[:-1], refs[-1]
    t, width = s_ref.shape
    choices = choice_ref[...]
    expert_at = lax.broadcasted_iota(jnp.int32, (t, 128), 1)
    first, second = expert_at == choices[:, 0:1], expert_at == choices[:, 1:2]
    earlier = lax.broadcasted_iota(jnp.int32, (t, t), 1) < lax.broadcasted_iota(
        jnp.int32, (t, t), 0
    )
    before = jnp.dot(
        earlier.astype(F32).astype(BF),
        (first | second).astype(F32).astype(BF),
        preferred_element_type=F32,
    ).astype(jnp.int32)
    keys = jnp.concatenate(
        [
            choices[:, k : k + 1] * 32
            + jnp.sum(jnp.where(named, before, 0), axis=1, keepdims=True)
            for k, named in enumerate((first, second))
        ],
        axis=0,
    )
    part = cap // len(returned)
    main, extra = part * 4 // 5, part // 5
    rows = experts * main
    at = lax.broadcasted_iota(jnp.int32, (1, rows), 1)
    quarter = width // 4
    picked = jnp.zeros((2 * t, width), F32)
    for c, back in enumerate(returned):
        main_key = at // main * 32 + c * part + at % main
        pick = (main_key == keys).astype(F32).astype(BF)
        picked += jnp.dot(pick, back[:, :width], preferred_element_type=F32)
        extra_key = at // main * 32 + c * part + main + at % main // 4
        parts = []
        for q in range(4):
            pick = ((extra_key == keys) & (at % 4 == q)).astype(F32).astype(BF)
            parts.append(jnp.dot(pick, back[:, width:], preferred_element_type=F32))
        picked += jnp.concatenate(parts, axis=1)
    gates = gate_ref[...]
    mixture = gates[:, 0:1] * picked[:t] + gates[:, 1:2] * picked[t:]
    o_ref[0] = (s_ref[...] + mixture).astype(BF)


def local(kernel, out_shape, scratch=(), **more):
    return pl.pallas_call(
        kernel,
        out_shape=out_shape,
        scratch_shapes=scratch,
        compiler_params=pltpu.CompilerParams(vmem_limit_bytes=LIMIT),
        **more,
    )


def run_experts(pieces, weight_in, weight_out, plus=()):
    rows, wide = pieces[0].shape
    hidden, width = weight_in.shape
    work = len(pieces) * rows * 5 // 4
    return local(
        functools.partial(expert_kernel, len(pieces)),
        [jax.ShapeDtypeStruct((rows, wide), BF)] * len(pieces),
        [pltpu.VMEM((work, width), BF)],
        cost_estimate=pl.CostEstimate(
            flops=4 * work * hidden * width,
            bytes_accessed=4 * hidden * width + 4 * len(pieces) * rows * wide,
            transcendentals=work * hidden,
        ),
    )(weight_in, weight_out, *pieces, *plus)


def add(*parts):
    return sum(p.astype(F32) for p in parts).astype(BF)


def shift(x, axis, by):
    n = lax.axis_size(axis)
    return lax.ppermute(x, axis, [(i, (i + by) % n) for i in range(n)])


def after(x, *others):
    return lax.optimization_barrier((x, *others))[0]


def ring_in(x):
    half = x.shape[0] // 2
    a, b = x[:half], x[half:]
    left_a, right_b = shift(a, "dp", 1), shift(b, "dp", -1)
    left_b, right_a = shift(b, "dp", 1), shift(a, "dp", -1)
    across_a, across_b = shift(left_a, "dp", 1), shift(right_b, "dp", -1)
    return (a, b), (left_a, left_b, right_a, right_b), (across_a, across_b)


def expert_layer(own, near, across, weights):
    to_left_a, to_left_b, to_right_a, to_right_b = run_experts(near, *weights)
    got_a, got_b = shift(to_left_a, "dp", -1), shift(to_right_b, "dp", 1)
    across = after(across, to_left_a)
    to_across_a, to_across_b = run_experts(across, *weights)
    via_a, via_b = shift(to_across_a, "dp", 1), shift(to_across_b, "dp", -1)
    via_a, via_b = add(to_right_a, via_a), add(to_left_b, via_b)
    sum_a, sum_b = shift(via_a, "dp", 1), shift(via_b, "dp", -1)
    own = after(own, via_a, via_b)
    own_a, own_b = run_experts(own, *weights, plus=(got_a, got_b))
    return jnp.concatenate([add(own_a, sum_a), add(own_b, sum_b)])


def per_device(
    projected,
    residual_in,
    modulation_scale,
    modulation_shift,
    expert_choice,
    gate_values,
    expert_in,
    expert_out,
):
    _, _, t, width = projected.shape
    n = lax.axis_size("ctx")
    experts = lax.axis_size("expert")
    cap = 5 * t * 2 // (4 * experts)
    slice_rows = expert_in.shape[1]
    packed = local(pack_kernel, jax.ShapeDtypeStruct((n, t * 9 // 2, 128), BF))(projected)
    block = local(join_kernel, jax.ShapeDtypeStruct((2 * slice_rows, width), BF))(
        expert_in, expert_out
    )
    mixed = lax.all_to_all(packed, "ctx", 0, 0, tiled=True)
    group = 4
    head_output = local(
        attend_kernel,
        jax.ShapeDtypeStruct((n, t * 3 // 2, 128), BF),
        [pltpu.VMEM((n * t, 128), BF)],
        grid=(n // group,),
        in_specs=[pl.BlockSpec((n, t * 9 // 2, 128), lambda i: (0, 0, 0))],
        out_specs=pl.BlockSpec((group, t * 3 // 2, 128), lambda i: (i, 0, 0)),
    )(mixed)
    back = lax.all_to_all(head_output, "ctx", 0, 0, tiled=True)
    part = cap // CHUNKS
    wide = (experts * part * 4 // 5, width * 5 // 4)
    stream, *sends = local(
        functools.partial(dispatch_kernel, experts, cap),
        [jax.ShapeDtypeStruct((t, width), F32)] + [jax.ShapeDtypeStruct(wide, BF)] * CHUNKS,
    )(back, residual_in[0], modulation_scale, modulation_shift, expert_choice[0].T)
    arrived = [lax.all_to_all(x, "expert", 0, 0, tiled=True) for x in sends]
    up, down = [shift(after(block, mixed), "ctx", 1)], [shift(after(block, mixed), "ctx", -1)]
    up[0], down[0] = after((up[0], down[0]), *sends)
    up.append(shift(up[-1], "ctx", 1))
    down.append(shift(down[-1], "ctx", -1))
    up[-1], down[-1] = local(
        relay_kernel,
        [jax.ShapeDtypeStruct(block.shape, BF)] * 2,
        cost_estimate=pl.CostEstimate(flops=10 * 10**9, bytes_accessed=0, transcendentals=0),
    )(up[-1], down[-1])
    *arrived, _, _ = lax.optimization_barrier((*arrived, up[-1], down[-1]))
    ring = ring_in(*arrived)
    up.append(shift(up[-1], "ctx", 1))
    down.append(shift(down[-1], "ctx", -1))
    up[-1], down[-1] = after((up[-1], down[-1]), ring[0])
    far_in = shift(up[-1][:slice_rows], "ctx", 1)
    far_out = shift(down[-1][slice_rows:], "ctx", -1)
    weights = local(
        assemble_kernel,
        [jax.ShapeDtypeStruct((n * slice_rows, width), BF)] * 2,

    )(far_in, far_out, block, *up, *down)
    sums = [expert_layer(*ring, weights)]
    returned = [lax.all_to_all(x, "expert", 0, 0, tiled=True) for x in sums]
    return local(
        functools.partial(combine_kernel, experts, cap),
        jax.ShapeDtypeStruct((1, t, width), BF),
    )(stream, expert_choice[0], gate_values[0], *returned)


def solution(mesh):
    return jax.shard_map(
        per_device,
        mesh=mesh,
        in_specs=(
            P(("dp", "expert"), None, "ctx", None),
            P(("dp", "expert"), "ctx", None),
            P(("dp", "expert"), None),
            P(("dp", "expert"), None),
            P(("dp", "expert"), "ctx", None),
            P(("dp", "expert"), "ctx", None),
            P("expert", ("dp", "ctx"), None),
            P("expert", ("dp", "ctx"), None),
        ),
        out_specs=P(("dp", "expert"), "ctx", None),
        check_vma=False,
    )
```

```python
import functools

import jax
import jax.numpy as jnp
from jax import lax
from jax.experimental import pallas as pl
from jax.experimental.pallas import tpu as pltpu
from jax.sharding import PartitionSpec as P

HD = 64
CHUNKS = 1
BF = jnp.bfloat16
F32 = jnp.float32
LIMIT = 24 * 1024 * 1024


def swap(x):
    return jnp.concatenate([x[:, HD:], x[:, :HD]], axis=1)


def low_lanes(rows):
    return lax.broadcasted_iota(jnp.int32, (rows, 2 * HD), 1) < HD


def join_kernel(in_ref, out_ref, w_ref):
    w_ref[: in_ref.shape[1], :] = in_ref[0]
    w_ref[in_ref.shape[1] :, :] = out_ref[0]


def pack_kernel(x_ref, o_ref):
    n = o_ref.shape[0]
    t = x_ref.shape[2]
    half = t // 2
    low, low_half = low_lanes(t), low_lanes(half)
    for j in range(n):
        for part in range(3):
            o_ref[j, part * t : (part + 1) * t, :] = x_ref[0, part, :, 128 * j : 128 * (j + 1)]
        at = 128 * (n + j // 2)
        q, k, v = (x_ref[0, part, :, at : at + 128] for part in range(3))
        if j % 2 == 0:
            o_ref[j, 3 * t : 4 * t, :] = jnp.where(low, q, swap(k))
            o_ref[j, 4 * t :, :] = jnp.where(low_half, v[:half], swap(v[half:]))
        else:
            o_ref[j, 3 * t : 4 * t, :] = jnp.where(low, swap(q), k)
            o_ref[j, 4 * t :, :] = jnp.where(low_half, swap(v[:half]), v[half:])


def attend_kernel(m_ref, o_ref, v2_ref):
    n, _, _ = m_ref.shape
    t = m_ref.shape[1] * 2 // 9
    half = t // 2
    group = o_ref.shape[0]
    step = pl.program_id(0)

    @pl.when(step == 0)
    def _():
        for z in range(n):
            block = m_ref[z, 4 * t :, :]
            v2_ref[z * t : z * t + half, :] = block
            v2_ref[z * t + half : (z + 1) * t, :] = swap(block)

    rows = group * t
    low = low_lanes(rows)
    mine = pl.ds(step * group, group)
    scaling = jnp.asarray(HD ** (-0.5), BF)
    q01 = m_ref[mine, 0:t, :].reshape(rows, 128) * scaling
    q2 = swap(m_ref[mine, 3 * t : 4 * t, :].reshape(rows, 128)) * scaling
    k01 = m_ref[:, t : 2 * t, :].reshape(n * t, 128)
    k2 = m_ref[:, 3 * t : 4 * t, :].reshape(n * t, 128)
    v01 = m_ref[:, 2 * t : 3 * t, :].reshape(n * t, 128)
    v2 = v2_ref[...]
    zero = jnp.zeros_like(q01)

    def head(q, k, v):
        scores = lax.dot_general(q, k, (((1,), (1,)), ((), ())), preferred_element_type=F32)
        probs = jnp.exp(scores - jnp.max(scores, axis=-1, keepdims=True))
        totals = jnp.sum(probs, axis=-1, keepdims=True)
        return jnp.dot(probs.astype(BF), v, preferred_element_type=F32) / totals

    a = head(jnp.where(low, q01, zero), k01, v01)
    b = head(jnp.where(low, zero, q01), k01, v01)
    c = head(jnp.where(low, zero, q2), k2, v2).astype(BF)
    pair = jnp.where(low, a, b).astype(BF)
    low_half = low_lanes(half)
    for g in range(group):
        o_ref[g, 0:t, :] = pair[g * t : (g + 1) * t]
        o_ref[g, t:, :] = jnp.where(
            low_half, c[g * t : g * t + half], swap(c[g * t + half : (g + 1) * t])
        )


def dispatch_kernel(experts, cap, b_ref, r_ref, scale_ref, shift_ref, choice_ref, s_ref, *sends):
    n = b_ref.shape[0]
    t, width = r_ref.shape
    half = t // 2
    low_half = low_lanes(half)
    tiles = [b_ref[j, 0:t, :] for j in range(n)]
    for m in range(n // 2):
        even, odd = b_ref[2 * m, t:, :], b_ref[2 * m + 1, t:, :]
        top = jnp.where(low_half, even, swap(odd))
        bottom = jnp.where(low_half, swap(even), odd)
        tiles.append(jnp.concatenate([top, bottom], axis=0))
    attended = jnp.concatenate(tiles, axis=1)
    stream = r_ref[...].astype(F32) + attended.astype(F32)
    s_ref[...] = stream
    mean_square = jnp.mean(stream * stream, axis=-1, keepdims=True)
    normed = (
        stream / jnp.sqrt(mean_square + 1e-06) * (1.0 + scale_ref[...]) + shift_ref[...]
    ).astype(BF)
    choices = choice_ref[...]
    expert_at = lax.broadcasted_iota(jnp.int32, (experts, t), 0)
    first, second = expert_at == choices[0:1], expert_at == choices[1:2]
    earlier = lax.broadcasted_iota(jnp.int32, (t, t), 0) < lax.broadcasted_iota(
        jnp.int32, (t, t), 1
    )
    before = jnp.dot(
        (first | second).astype(F32).astype(BF),
        earlier.astype(F32).astype(BF),
        preferred_element_type=F32,
    ).astype(jnp.int32)
    keys = [
        choices[k : k + 1] * 32 + jnp.sum(jnp.where(named, before, 0), axis=0, keepdims=True)
        for k, named in enumerate((first, second))
    ]
    part = cap // len(sends)
    main, extra = part * 4 // 5, part // 5
    rows = experts * main
    at = lax.broadcasted_iota(jnp.int32, (rows, 1), 0)
    quarter = width // 4
    for c, send in enumerate(sends):
        main_key = at // main * 32 + c * part + at % main
        pick = ((main_key == keys[0]) | (main_key == keys[1])).astype(F32).astype(BF)
        send[:, :width] = jnp.dot(pick, normed, preferred_element_type=F32).astype(BF)
        extra_key = at // main * 32 + c * part + main + at % main // 4
        matches = (extra_key == keys[0]) | (extra_key == keys[1])
        total = jnp.zeros((rows, quarter), F32)
        for q in range(4):
            pick = (matches & (at % 4 == q)).astype(F32).astype(BF)
            total += jnp.dot(
                pick, normed[:, q * quarter : (q + 1) * quarter], preferred_element_type=F32
            )
        send[:, width:] = total.astype(BF)


def assemble_kernel(*refs):
    far_in, far_out, *blocks, in_ref, out_ref = refs
    rows = far_in.shape[0]
    in_ref[len(blocks) * rows :, :] = far_in[...]
    out_ref[len(blocks) * rows :, :] = far_out[...]
    for i, block in enumerate(blocks):
        in_ref[i * rows : (i + 1) * rows, :] = block[:rows, :]
        out_ref[i * rows : (i + 1) * rows, :] = block[rows:, :]


def relay_kernel(up_ref, down_ref, up_out_ref, down_out_ref):
    up_out_ref[...] = up_ref[...]
    down_out_ref[...] = down_ref[...]


def expert_kernel(pieces, in_ref, out_ref, *refs):
    x_refs, plus, y_refs, rows_ref = refs[:pieces], refs[pieces : -pieces - 1], refs[-pieces - 1 : -1], refs[-1]
    rows = x_refs[0].shape[0]
    width = in_ref.shape[1]
    quarter = width // 4
    extras = rows // 4
    every = rows + extras
    row_at = lax.broadcasted_iota(jnp.int32, (rows, rows), 0)
    source = lax.broadcasted_iota(jnp.int32, (rows, rows), 1)
    pick = (source == 4 * (row_at % extras) + row_at // extras).astype(F32).astype(BF)
    for p, x_ref in enumerate(x_refs):
        base = p * every
        rows_ref[base : base + rows, :] = x_ref[:, :width]
        quarters = jnp.dot(pick, x_ref[:, width:], preferred_element_type=F32).astype(BF)
        for q in range(4):
            rows_ref[base + rows : base + every, q * quarter : (q + 1) * quarter] = quarters[
                q * extras : (q + 1) * extras
            ]
    pre_act = lax.dot_general(
        rows_ref[...], in_ref[...], (((1,), (1,)), ((), ())), preferred_element_type=F32
    )
    hidden = jax.nn.gelu(pre_act, approximate=True).astype(BF)
    partial = jnp.dot(hidden, out_ref[...], preferred_element_type=F32).astype(BF)
    pack = (row_at == 4 * (source % extras) + source // extras).astype(F32).astype(BF)
    for p, y_ref in enumerate(y_refs):
        base = p * every
        main = partial[base : base + rows]
        last = partial[base + rows : base + every]
        quarters = jnp.concatenate(
            [last[:, q * quarter : (q + 1) * quarter] for q in range(4)], axis=0
        )
        total = jnp.dot(pack, quarters, preferred_element_type=F32).astype(BF)
        if plus:
            main = add(main, plus[p][:, :width])
            total = add(total, plus[p][:, width:])
        y_ref[:, :width] = main
        y_ref[:, width:] = total


def combine_kernel(experts, cap, s_ref, choice_ref, gate_ref, *refs):
    returned, o_ref = refs[:-1], refs[-1]
    t, width = s_ref.shape
    choices = choice_ref[...]
    expert_at = lax.broadcasted_iota(jnp.int32, (t, 128), 1)
    first, second = expert_at == choices[:, 0:1], expert_at == choices[:, 1:2]
    earlier = lax.broadcasted_iota(jnp.int32, (t, t), 1) < lax.broadcasted_iota(
        jnp.int32, (t, t), 0
    )
    before = jnp.dot(
        earlier.astype(F32).astype(BF),
        (first | second).astype(F32).astype(BF),
        preferred_element_type=F32,
    ).astype(jnp.int32)
    keys = jnp.concatenate(
        [
            choices[:, k : k + 1] * 32
            + jnp.sum(jnp.where(named, before, 0), axis=1, keepdims=True)
            for k, named in enumerate((first, second))
        ],
        axis=0,
    )
    part = cap // len(returned)
    main, extra = part * 4 // 5, part // 5
    rows = experts * main
    at = lax.broadcasted_iota(jnp.int32, (1, rows), 1)
    quarter = width // 4
    picked = jnp.zeros((2 * t, width), F32)
    for c, back in enumerate(returned):
        main_key = at // main * 32 + c * part + at % main
        pick = (main_key == keys).astype(F32).astype(BF)
        picked += jnp.dot(pick, back[:, :width], preferred_element_type=F32)
        extra_key = at // main * 32 + c * part + main + at % main // 4
        parts = []
        for q in range(4):
            pick = ((extra_key == keys) & (at % 4 == q)).astype(F32).astype(BF)
            parts.append(jnp.dot(pick, back[:, width:], preferred_element_type=F32))
        picked += jnp.concatenate(parts, axis=1)
    gates = gate_ref[...]
    mixture = gates[:, 0:1] * picked[:t] + gates[:, 1:2] * picked[t:]
    o_ref[0] = (s_ref[...] + mixture).astype(BF)


def local(kernel, out_shape, scratch=(), **more):
    return pl.pallas_call(
        kernel,
        out_shape=out_shape,
        scratch_shapes=scratch,
        compiler_params=pltpu.CompilerParams(vmem_limit_bytes=LIMIT),
        **more,
    )


def run_experts(pieces, weight_in, weight_out, plus=()):
    rows, wide = pieces[0].shape
    hidden, width = weight_in.shape
    work = len(pieces) * rows * 5 // 4
    return local(
        functools.partial(expert_kernel, len(pieces)),
        [jax.ShapeDtypeStruct((rows, wide), BF)] * len(pieces),
        [pltpu.VMEM((work, width), BF)],
        cost_estimate=pl.CostEstimate(
            flops=4 * work * hidden * width,
            bytes_accessed=4 * hidden * width + 4 * len(pieces) * rows * wide,
            transcendentals=work * hidden,
        ),
    )(weight_in, weight_out, *pieces, *plus)


def add(*parts):
    return sum(p.astype(F32) for p in parts).astype(BF)


def shift(x, axis, by):
    n = lax.axis_size(axis)
    return lax.ppermute(x, axis, [(i, (i + by) % n) for i in range(n)])


def after(x, *others):
    return lax.optimization_barrier((x, *others))[0]


def ring_in(x):
    half = x.shape[0] // 2
    a, b = x[:half], x[half:]
    left_a, right_b = shift(a, "dp", 1), shift(b, "dp", -1)
    left_b, right_a = shift(b, "dp", 1), shift(a, "dp", -1)
    across_a, across_b = shift(left_a, "dp", 1), shift(right_b, "dp", -1)
    left_b, right_a = local(
        relay_kernel,
        [jax.ShapeDtypeStruct(a.shape, BF)] * 2,
        cost_estimate=pl.CostEstimate(flops=3 * 10**9, bytes_accessed=0, transcendentals=0),
    )(left_b, right_a)
    return (a, b), (left_a, left_b, right_a, right_b), (across_a, across_b)


def expert_layer(own, near, across, weights):
    to_left_a, to_left_b, to_right_a, to_right_b = run_experts(near, *weights)
    got_a, got_b = shift(to_left_a, "dp", -1), shift(to_right_b, "dp", 1)
    across = after(across, to_left_a)
    to_across_a, to_across_b = run_experts(across, *weights)
    via_a, via_b = shift(to_across_a, "dp", 1), shift(to_across_b, "dp", -1)
    via_a, via_b = add(to_right_a, via_a), add(to_left_b, via_b)
    sum_a, sum_b = shift(via_a, "dp", 1), shift(via_b, "dp", -1)
    own = after(own, via_a, via_b)
    own_a, own_b = run_experts(own, *weights, plus=(got_a, got_b))
    return jnp.concatenate([add(own_a, sum_a), add(own_b, sum_b)])


def per_device(
    projected,
    residual_in,
    modulation_scale,
    modulation_shift,
    expert_choice,
    gate_values,
    expert_in,
    expert_out,
):
    _, _, t, width = projected.shape
    n = lax.axis_size("ctx")
    experts = lax.axis_size("expert")
    cap = 5 * t * 2 // (4 * experts)
    slice_rows = expert_in.shape[1]
    packed = local(pack_kernel, jax.ShapeDtypeStruct((n, t * 9 // 2, 128), BF))(projected)
    block = local(join_kernel, jax.ShapeDtypeStruct((2 * slice_rows, width), BF))(
        expert_in, expert_out
    )
    mixed = lax.all_to_all(packed, "ctx", 0, 0, tiled=True)
    group = 4
    head_output = local(
        attend_kernel,
        jax.ShapeDtypeStruct((n, t * 3 // 2, 128), BF),
        [pltpu.VMEM((n * t, 128), BF)],
        grid=(n // group,),
        in_specs=[pl.BlockSpec((n, t * 9 // 2, 128), lambda i: (0, 0, 0))],
        out_specs=pl.BlockSpec((group, t * 3 // 2, 128), lambda i: (i, 0, 0)),
    )(mixed)
    back = lax.all_to_all(head_output, "ctx", 0, 0, tiled=True)
    part = cap // CHUNKS
    wide = (experts * part * 4 // 5, width * 5 // 4)
    stream, *sends = local(
        functools.partial(dispatch_kernel, experts, cap),
        [jax.ShapeDtypeStruct((t, width), F32)] + [jax.ShapeDtypeStruct(wide, BF)] * CHUNKS,
    )(back, residual_in[0], modulation_scale, modulation_shift, expert_choice[0].T)
    arrived = [lax.all_to_all(x, "expert", 0, 0, tiled=True) for x in sends]
    up, down = [shift(after(block, mixed), "ctx", 1)], [shift(after(block, mixed), "ctx", -1)]
    up[0], down[0] = after((up[0], down[0]), *sends)
    up.append(shift(up[-1], "ctx", 1))
    down.append(shift(down[-1], "ctx", -1))
    up[-1], down[-1] = local(
        relay_kernel,
        [jax.ShapeDtypeStruct(block.shape, BF)] * 2,
        cost_estimate=pl.CostEstimate(flops=10 * 10**9, bytes_accessed=0, transcendentals=0),
    )(up[-1], down[-1])
    *arrived, _, _ = lax.optimization_barrier((*arrived, up[-1], down[-1]))
    ring = ring_in(*arrived)
    up.append(shift(up[-1], "ctx", 1))
    down.append(shift(down[-1], "ctx", -1))
    up[-1], down[-1] = after((up[-1], down[-1]), *ring[1][::3])
    far_in = shift(up[-1][:slice_rows], "ctx", 1)
    far_out = shift(down[-1][slice_rows:], "ctx", -1)
    weights = local(
        assemble_kernel,
        [jax.ShapeDtypeStruct((n * slice_rows, width), BF)] * 2,

    )(far_in, far_out, block, *up, *down)
    sums = [expert_layer(*ring, weights)]
    returned = [lax.all_to_all(x, "expert", 0, 0, tiled=True) for x in sums]
    return local(
        functools.partial(combine_kernel, experts, cap),
        jax.ShapeDtypeStruct((1, t, width), BF),
    )(stream, expert_choice[0], gate_values[0], *returned)


def solution(mesh):
    return jax.shard_map(
        per_device,
        mesh=mesh,
        in_specs=(
            P(("dp", "expert"), None, "ctx", None),
            P(("dp", "expert"), "ctx", None),
            P(("dp", "expert"), None),
            P(("dp", "expert"), None),
            P(("dp", "expert"), "ctx", None),
            P(("dp", "expert"), "ctx", None),
            P("expert", ("dp", "ctx"), None),
            P("expert", ("dp", "ctx"), None),
        ),
        out_specs=P(("dp", "expert"), "ctx", None),
        check_vma=False,
    )
```

```python
import functools

import jax
import jax.numpy as jnp
from jax import lax
from jax.experimental import pallas as pl
from jax.experimental.pallas import tpu as pltpu
from jax.sharding import PartitionSpec as P

HD = 64
CHUNKS = 1
BF = jnp.bfloat16
F32 = jnp.float32
LIMIT = 24 * 1024 * 1024


def swap(x):
    return jnp.concatenate([x[:, HD:], x[:, :HD]], axis=1)


def low_lanes(rows):
    return lax.broadcasted_iota(jnp.int32, (rows, 2 * HD), 1) < HD


def join_kernel(in_ref, out_ref, w_ref):
    w_ref[: in_ref.shape[1], :] = in_ref[0]
    w_ref[in_ref.shape[1] :, :] = out_ref[0]


def pack_kernel(x_ref, o_ref):
    n = o_ref.shape[0]
    t = x_ref.shape[2]
    half = t // 2
    low, low_half = low_lanes(t), low_lanes(half)
    for j in range(n):
        for part in range(3):
            o_ref[j, part * t : (part + 1) * t, :] = x_ref[0, part, :, 128 * j : 128 * (j + 1)]
        at = 128 * (n + j // 2)
        q, k, v = (x_ref[0, part, :, at : at + 128] for part in range(3))
        if j % 2 == 0:
            o_ref[j, 3 * t : 4 * t, :] = jnp.where(low, q, swap(k))
            o_ref[j, 4 * t :, :] = jnp.where(low_half, v[:half], swap(v[half:]))
        else:
            o_ref[j, 3 * t : 4 * t, :] = jnp.where(low, swap(q), k)
            o_ref[j, 4 * t :, :] = jnp.where(low_half, swap(v[:half]), v[half:])


def attend_kernel(m_ref, o_ref, v2_ref):
    n, _, _ = m_ref.shape
    t = m_ref.shape[1] * 2 // 9
    half = t // 2
    group = o_ref.shape[0]
    step = pl.program_id(0)

    @pl.when(step == 0)
    def _():
        for z in range(n):
            block = m_ref[z, 4 * t :, :]
            v2_ref[z * t : z * t + half, :] = block
            v2_ref[z * t + half : (z + 1) * t, :] = swap(block)

    rows = group * t
    low = low_lanes(rows)
    mine = pl.ds(step * group, group)
    scaling = jnp.asarray(HD ** (-0.5), BF)
    q01 = m_ref[mine, 0:t, :].reshape(rows, 128) * scaling
    q2 = swap(m_ref[mine, 3 * t : 4 * t, :].reshape(rows, 128)) * scaling
    k01 = m_ref[:, t : 2 * t, :].reshape(n * t, 128)
    k2 = m_ref[:, 3 * t : 4 * t, :].reshape(n * t, 128)
    v01 = m_ref[:, 2 * t : 3 * t, :].reshape(n * t, 128)
    v2 = v2_ref[...]
    zero = jnp.zeros_like(q01)

    def head(q, k, v):
        scores = lax.dot_general(q, k, (((1,), (1,)), ((), ())), preferred_element_type=F32)
        probs = jnp.exp(scores - jnp.max(scores, axis=-1, keepdims=True))
        totals = jnp.sum(probs, axis=-1, keepdims=True)
        return jnp.dot(probs.astype(BF), v, preferred_element_type=F32) / totals

    a = head(jnp.where(low, q01, zero), k01, v01)
    b = head(jnp.where(low, zero, q01), k01, v01)
    c = head(jnp.where(low, zero, q2), k2, v2).astype(BF)
    pair = jnp.where(low, a, b).astype(BF)
    low_half = low_lanes(half)
    for g in range(group):
        o_ref[g, 0:t, :] = pair[g * t : (g + 1) * t]
        o_ref[g, t:, :] = jnp.where(
            low_half, c[g * t : g * t + half], swap(c[g * t + half : (g + 1) * t])
        )


def dispatch_kernel(experts, cap, b_ref, r_ref, scale_ref, shift_ref, choice_ref, s_ref, *sends):
    n = b_ref.shape[0]
    t, width = r_ref.shape
    half = t // 2
    low_half = low_lanes(half)
    tiles = [b_ref[j, 0:t, :] for j in range(n)]
    for m in range(n // 2):
        even, odd = b_ref[2 * m, t:, :], b_ref[2 * m + 1, t:, :]
        top = jnp.where(low_half, even, swap(odd))
        bottom = jnp.where(low_half, swap(even), odd)
        tiles.append(jnp.concatenate([top, bottom], axis=0))
    attended = jnp.concatenate(tiles, axis=1)
    stream = r_ref[...].astype(F32) + attended.astype(F32)
    s_ref[...] = stream
    mean_square = jnp.mean(stream * stream, axis=-1, keepdims=True)
    normed = (
        stream / jnp.sqrt(mean_square + 1e-06) * (1.0 + scale_ref[...]) + shift_ref[...]
    ).astype(BF)
    choices = choice_ref[...]
    expert_at = lax.broadcasted_iota(jnp.int32, (experts, t), 0)
    first, second = expert_at == choices[0:1], expert_at == choices[1:2]
    earlier = lax.broadcasted_iota(jnp.int32, (t, t), 0) < lax.broadcasted_iota(
        jnp.int32, (t, t), 1
    )
    before = jnp.dot(
        (first | second).astype(F32).astype(BF),
        earlier.astype(F32).astype(BF),
        preferred_element_type=F32,
    ).astype(jnp.int32)
    keys = [
        choices[k : k + 1] * 32 + jnp.sum(jnp.where(named, before, 0), axis=0, keepdims=True)
        for k, named in enumerate((first, second))
    ]
    part = cap // len(sends)
    main, extra = part * 4 // 5, part // 5
    rows = experts * main
    at = lax.broadcasted_iota(jnp.int32, (rows, 1), 0)
    quarter = width // 4
    for c, send in enumerate(sends):
        main_key = at // main * 32 + c * part + at % main
        pick = ((main_key == keys[0]) | (main_key == keys[1])).astype(F32).astype(BF)
        send[:, :width] = jnp.dot(pick, normed, preferred_element_type=F32).astype(BF)
        extra_key = at // main * 32 + c * part + main + at % main // 4
        matches = (extra_key == keys[0]) | (extra_key == keys[1])
        total = jnp.zeros((rows, quarter), F32)
        for q in range(4):
            pick = (matches & (at % 4 == q)).astype(F32).astype(BF)
            total += jnp.dot(
                pick, normed[:, q * quarter : (q + 1) * quarter], preferred_element_type=F32
            )
        send[:, width:] = total.astype(BF)


def assemble_kernel(*refs):
    far_in, far_out, *blocks, in_ref, out_ref = refs
    rows = far_in.shape[0]
    in_ref[len(blocks) * rows :, :] = far_in[...]
    out_ref[len(blocks) * rows :, :] = far_out[...]
    for i, block in enumerate(blocks):
        in_ref[i * rows : (i + 1) * rows, :] = block[:rows, :]
        out_ref[i * rows : (i + 1) * rows, :] = block[rows:, :]


def relay_kernel(up_ref, down_ref, up_out_ref, down_out_ref):
    up_out_ref[...] = up_ref[...]
    down_out_ref[...] = down_ref[...]


def expert_kernel(pieces, in_ref, out_ref, *refs):
    x_refs, plus, y_refs, rows_ref = refs[:pieces], refs[pieces : -pieces - 1], refs[-pieces - 1 : -1], refs[-1]
    rows = x_refs[0].shape[0]
    width = in_ref.shape[1]
    quarter = width // 4
    extras = rows // 4
    every = rows + extras
    row_at = lax.broadcasted_iota(jnp.int32, (rows, rows), 0)
    source = lax.broadcasted_iota(jnp.int32, (rows, rows), 1)
    pick = (source == 4 * (row_at % extras) + row_at // extras).astype(F32).astype(BF)
    for p, x_ref in enumerate(x_refs):
        base = p * every
        rows_ref[base : base + rows, :] = x_ref[:, :width]
        quarters = jnp.dot(pick, x_ref[:, width:], preferred_element_type=F32).astype(BF)
        for q in range(4):
            rows_ref[base + rows : base + every, q * quarter : (q + 1) * quarter] = quarters[
                q * extras : (q + 1) * extras
            ]
    pre_act = lax.dot_general(
        rows_ref[...], in_ref[...], (((1,), (1,)), ((), ())), preferred_element_type=F32
    )
    hidden = jax.nn.gelu(pre_act, approximate=True).astype(BF)
    partial = jnp.dot(hidden, out_ref[...], preferred_element_type=F32).astype(BF)
    pack = (row_at == 4 * (source % extras) + source // extras).astype(F32).astype(BF)
    for p, y_ref in enumerate(y_refs):
        base = p * every
        main = partial[base : base + rows]
        last = partial[base + rows : base + every]
        quarters = jnp.concatenate(
            [last[:, q * quarter : (q + 1) * quarter] for q in range(4)], axis=0
        )
        total = jnp.dot(pack, quarters, preferred_element_type=F32).astype(BF)
        if plus:
            main = add(main, plus[p][:, :width])
            total = add(total, plus[p][:, width:])
        y_ref[:, :width] = main
        y_ref[:, width:] = total


def combine_kernel(experts, cap, s_ref, choice_ref, gate_ref, *refs):
    returned, o_ref = refs[:-1], refs[-1]
    t, width = s_ref.shape
    choices = choice_ref[...]
    expert_at = lax.broadcasted_iota(jnp.int32, (t, 128), 1)
    first, second = expert_at == choices[:, 0:1], expert_at == choices[:, 1:2]
    earlier = lax.broadcasted_iota(jnp.int32, (t, t), 1) < lax.broadcasted_iota(
        jnp.int32, (t, t), 0
    )
    before = jnp.dot(
        earlier.astype(F32).astype(BF),
        (first | second).astype(F32).astype(BF),
        preferred_element_type=F32,
    ).astype(jnp.int32)
    keys = jnp.concatenate(
        [
            choices[:, k : k + 1] * 32
            + jnp.sum(jnp.where(named, before, 0), axis=1, keepdims=True)
            for k, named in enumerate((first, second))
        ],
        axis=0,
    )
    part = cap // len(returned)
    main, extra = part * 4 // 5, part // 5
    rows = experts * main
    at = lax.broadcasted_iota(jnp.int32, (1, rows), 1)
    quarter = width // 4
    picked = jnp.zeros((2 * t, width), F32)
    for c, back in enumerate(returned):
        main_key = at // main * 32 + c * part + at % main
        pick = (main_key == keys).astype(F32).astype(BF)
        picked += jnp.dot(pick, back[:, :width], preferred_element_type=F32)
        extra_key = at // main * 32 + c * part + main + at % main // 4
        parts = []
        for q in range(4):
            pick = ((extra_key == keys) & (at % 4 == q)).astype(F32).astype(BF)
            parts.append(jnp.dot(pick, back[:, width:], preferred_element_type=F32))
        picked += jnp.concatenate(parts, axis=1)
    gates = gate_ref[...]
    mixture = gates[:, 0:1] * picked[:t] + gates[:, 1:2] * picked[t:]
    o_ref[0] = (s_ref[...] + mixture).astype(BF)


def local(kernel, out_shape, scratch=(), **more):
    return pl.pallas_call(
        kernel,
        out_shape=out_shape,
        scratch_shapes=scratch,
        compiler_params=pltpu.CompilerParams(vmem_limit_bytes=LIMIT),
        **more,
    )


def run_experts(pieces, weight_in, weight_out, plus=()):
    rows, wide = pieces[0].shape
    hidden, width = weight_in.shape
    work = len(pieces) * rows * 5 // 4
    return local(
        functools.partial(expert_kernel, len(pieces)),
        [jax.ShapeDtypeStruct((rows, wide), BF)] * len(pieces),
        [pltpu.VMEM((work, width), BF)],
        cost_estimate=pl.CostEstimate(
            flops=4 * work * hidden * width,
            bytes_accessed=4 * hidden * width + 4 * len(pieces) * rows * wide,
            transcendentals=work * hidden,
        ),
    )(weight_in, weight_out, *pieces, *plus)


def add(*parts):
    return sum(p.astype(F32) for p in parts).astype(BF)


def shift(x, axis, by):
    n = lax.axis_size(axis)
    return lax.ppermute(x, axis, [(i, (i + by) % n) for i in range(n)])


def after(x, *others):
    return lax.optimization_barrier((x, *others))[0]


def ring_in(x):
    half = x.shape[0] // 2
    a, b = x[:half], x[half:]
    left_a, right_b = shift(a, "dp", 1), shift(b, "dp", -1)
    left_b, right_a = shift(b, "dp", 1), shift(a, "dp", -1)
    across_a, across_b = shift(left_a, "dp", 1), shift(right_b, "dp", -1)
    left_b, right_a = local(
        relay_kernel,
        [jax.ShapeDtypeStruct(a.shape, BF)] * 2,
        cost_estimate=pl.CostEstimate(flops=3 * 10**9, bytes_accessed=0, transcendentals=0),
    )(left_b, right_a)
    return (a, b), (left_a, left_b, right_a, right_b), (across_a, across_b)


def expert_layer(own, near, across, weights):
    to_left_a, to_left_b, to_right_a, to_right_b = run_experts(near, *weights)
    got_a, got_b = local(
        relay_kernel,
        [jax.ShapeDtypeStruct(to_left_a.shape, BF)] * 2,
        cost_estimate=pl.CostEstimate(flops=12 * 10**9, bytes_accessed=0, transcendentals=0),
    )(shift(to_left_a, "dp", -1), shift(to_right_b, "dp", 1))
    across = after(across, to_left_a)
    to_across_a, to_across_b = run_experts(across, *weights)
    via_a, via_b = shift(to_across_a, "dp", 1), shift(to_across_b, "dp", -1)
    via_a, via_b = add(to_right_a, via_a), add(to_left_b, via_b)
    sum_a, sum_b = shift(via_a, "dp", 1), shift(via_b, "dp", -1)
    own = after(own, via_a, via_b)
    own_a, own_b = run_experts(own, *weights, plus=(got_a, got_b))
    return jnp.concatenate([add(own_a, sum_a), add(own_b, sum_b)])


def per_device(
    projected,
    residual_in,
    modulation_scale,
    modulation_shift,
    expert_choice,
    gate_values,
    expert_in,
    expert_out,
):
    _, _, t, width = projected.shape
    n = lax.axis_size("ctx")
    experts = lax.axis_size("expert")
    cap = 5 * t * 2 // (4 * experts)
    slice_rows = expert_in.shape[1]
    packed = local(pack_kernel, jax.ShapeDtypeStruct((n, t * 9 // 2, 128), BF))(projected)
    block = local(join_kernel, jax.ShapeDtypeStruct((2 * slice_rows, width), BF))(
        expert_in, expert_out
    )
    mixed = lax.all_to_all(packed, "ctx", 0, 0, tiled=True)
    group = 4
    head_output = local(
        attend_kernel,
        jax.ShapeDtypeStruct((n, t * 3 // 2, 128), BF),
        [pltpu.VMEM((n * t, 128), BF)],
        grid=(n // group,),
        in_specs=[pl.BlockSpec((n, t * 9 // 2, 128), lambda i: (0, 0, 0))],
        out_specs=pl.BlockSpec((group, t * 3 // 2, 128), lambda i: (i, 0, 0)),
    )(mixed)
    back = lax.all_to_all(head_output, "ctx", 0, 0, tiled=True)
    part = cap // CHUNKS
    wide = (experts * part * 4 // 5, width * 5 // 4)
    stream, *sends = local(
        functools.partial(dispatch_kernel, experts, cap),
        [jax.ShapeDtypeStruct((t, width), F32)] + [jax.ShapeDtypeStruct(wide, BF)] * CHUNKS,
    )(back, residual_in[0], modulation_scale, modulation_shift, expert_choice[0].T)
    arrived = [lax.all_to_all(x, "expert", 0, 0, tiled=True) for x in sends]
    up, down = [shift(after(block, mixed), "ctx", 1)], [shift(after(block, mixed), "ctx", -1)]
    up[0], down[0] = after((up[0], down[0]), *sends)
    up.append(shift(up[-1], "ctx", 1))
    down.append(shift(down[-1], "ctx", -1))
    up[-1], down[-1] = local(
        relay_kernel,
        [jax.ShapeDtypeStruct(block.shape, BF)] * 2,
        cost_estimate=pl.CostEstimate(flops=10 * 10**9, bytes_accessed=0, transcendentals=0),
    )(up[-1], down[-1])
    *arrived, _, _ = lax.optimization_barrier((*arrived, up[-1], down[-1]))
    ring = ring_in(*arrived)
    up.append(shift(up[-1], "ctx", 1))
    down.append(shift(down[-1], "ctx", -1))
    up[-1], down[-1] = after((up[-1], down[-1]), *ring[1][::3])
    far_in = shift(up[-1][:slice_rows], "ctx", 1)
    far_out = shift(down[-1][slice_rows:], "ctx", -1)
    weights = local(
        assemble_kernel,
        [jax.ShapeDtypeStruct((n * slice_rows, width), BF)] * 2,

    )(far_in, far_out, block, *up, *down)
    sums = [expert_layer(*ring, weights)]
    returned = [lax.all_to_all(x, "expert", 0, 0, tiled=True) for x in sums]
    return local(
        functools.partial(combine_kernel, experts, cap),
        jax.ShapeDtypeStruct((1, t, width), BF),
    )(stream, expert_choice[0], gate_values[0], *returned)


def solution(mesh):
    return jax.shard_map(
        per_device,
        mesh=mesh,
        in_specs=(
            P(("dp", "expert"), None, "ctx", None),
            P(("dp", "expert"), "ctx", None),
            P(("dp", "expert"), None),
            P(("dp", "expert"), None),
            P(("dp", "expert"), "ctx", None),
            P(("dp", "expert"), "ctx", None),
            P("expert", ("dp", "ctx"), None),
            P("expert", ("dp", "ctx"), None),
        ),
        out_specs=P(("dp", "expert"), "ctx", None),
        check_vma=False,
    )
```
